512 devices in a mesh: owner: 32 (over x, z_hi, core), panel: 16 (over z_lo, y).
Axes of the slice: x: 4, y: 8, z: 8 (z_hi: 4, z_lo: 2; z = z_hi * 2 + z_lo), core: 2. Of those that a mesh axis runs over, the one named last changes fastest.
Arguments:
- embeddings: bfloat16 [114688, 1024], P(('owner', 'panel')), may hold values from -256 to 256
- cluster_id: int32 [114688], P(('owner', 'panel')), may hold values from 0 to 511, as said below
- row_index: int32 [114688], P(('owner', 'panel')), may hold values from 0 to 114687, each once
Outputs:
- best_match: float32 [114688], P(('owner', 'panel'))
The draws below stay inside these ranges and needn't reach their ends.
Inputs may be any that keep to these rules, and one draw needn't show every extreme that they name: `cluster_id`: in each aligned block of 224 rows, at most 14 rows have cluster ids with one same remainder modulo 32, and in every block some remainder has exactly 14 rows. `row_index`: each global index appears once.
All inputs are finite; a program needn't handle non-finite values.
Results may differ from the reference program's by a relative error of at most 0.00048.
Values may be sent and summed in bfloat16 or wider, within the bound.
A program may use at most 64 MiB of HBM per device.

```python
import math
import jax
import jax.numpy as jnp
from jax import lax

D = 1024
ROWS_DEV = 224
CLU_OWN = 16
CAP = 14
ROWS = 114688
CLUSTERS = 512
N_OWNER = 32


def row_layout(key):
    block_count = ROWS // ROWS_DEV

    def per_block(block_key):
        key_full, key_pick, key_order = jax.random.split(block_key, 3)
        full_owner = jax.random.randint(key_full, (), 0, N_OWNER)
        others = (full_owner + 1 + jnp.arange((N_OWNER - 1) * CAP) // CAP) % N_OWNER
        chosen = jax.random.permutation(key_pick, others)[:ROWS_DEV - CAP]
        owners_list = jnp.concatenate([jnp.full((CAP,), full_owner, jnp.int32), chosen.astype(jnp.int32)])
        return jax.random.permutation(key_order, owners_list)
    owner_rows = jax.vmap(per_block)(jax.random.split(key, block_count)).reshape(-1)
    key_heavy, key_pick_local, key_bucket = jax.random.split(jax.random.fold_in(key, 11), 3)
    heavy_local = jax.random.randint(key_heavy, (N_OWNER,), 0, CLU_OWN).astype(jnp.int32)
    drawn = jax.random.randint(key_pick_local, (ROWS,), 0, 2 * CLU_OWN).astype(jnp.int32)
    local_index = jnp.where(drawn < CLU_OWN, heavy_local[owner_rows], drawn - CLU_OWN)
    cluster = (owner_rows + N_OWNER * local_index).astype(jnp.int32)
    bucket = jax.random.randint(key_bucket, (ROWS,), 0, 64).astype(jnp.int32)
    return (cluster, bucket)


def draw_cluster_id(key, part):
    cluster, bucket = row_layout(key)
    return cluster


def draw_embeddings(key, part):
    cluster, bucket = row_layout(key)
    key = jax.random.fold_in(key, 5)
    key_centre, key_shared, key_pull, key_duplicate, key_noise = jax.random.split(key, 5)
    centre = jnp.clip(jax.random.normal(key_centre, (CLUSTERS, D), jnp.float32), -4.0, 4.0)
    shared = jnp.clip(jax.random.normal(key_shared, (CLUSTERS * 64, D), jnp.float32), -4.0, 4.0)
    centre_pull = jnp.exp(jax.random.uniform(key_pull, (CLUSTERS,), jnp.float32, math.log(0.3), math.log(1.5)))
    duplicate = jax.random.uniform(key_duplicate, (ROWS, 1), jnp.float32, 0.0, 3.0)
    noise_part = jnp.clip(jax.random.normal(key_noise, (ROWS, D), jnp.float32), -4.0, 4.0)
    values = centre_pull[cluster][:, None] * centre[cluster] + duplicate * shared[cluster * 64 + bucket] + noise_part
    return values.astype(jnp.bfloat16)


def setup_inputs(seed: int = 0) -> dict:
    keys = jax.random.split(jax.random.key(seed), 4)
    embeddings = draw_embeddings(jax.random.fold_in(keys[3], 71), 0)
    cluster_id = draw_cluster_id(jax.random.fold_in(keys[3], 71), 0)
    row_index = jax.random.permutation(keys[2], ROWS).astype(jnp.int32)
    return {"embeddings": embeddings, "cluster_id": cluster_id, "row_index": row_index}


def reference(embeddings, cluster_id, row_index):
    widened = embeddings.astype(jnp.float32)
    square_sum = lax.optimization_barrier(jnp.sum(widened * widened, axis=1, keepdims=True))
    inverse_norm = lax.rsqrt(square_sum + 1e-06)
    unit_rows = (widened * inverse_norm).astype(jnp.bfloat16)
    row_total = embeddings.shape[0]
    row_keys = (cluster_id * row_total + row_index).astype(jnp.int32)
    owner_group = (cluster_id % N_OWNER).astype(jnp.int32)
    ordering = jnp.argsort(owner_group, stable=True).astype(jnp.int32)
    group_sizes = lax.optimization_barrier(jnp.sum((owner_group[:, None] == jnp.arange(N_OWNER, dtype=jnp.int32)[None, :]).astype(jnp.int32), axis=0))
    group_starts = (jnp.cumsum(group_sizes) - group_sizes).astype(jnp.int32)
    group_width = CAP * (ROWS // ROWS_DEV)
    block_width = 2 * ROWS_DEV
    padded_order = jnp.concatenate([ordering, jnp.full((group_width,), row_total, jnp.int32)])

    def per_group(group_number):
        offsets = jnp.arange(group_width, dtype=jnp.int32)
        positions = (group_starts[group_number] + offsets).astype(jnp.int32)
        members = jnp.where(offsets < group_sizes[group_number], padded_order[positions], row_total).astype(jnp.int32)
        safe_members = jnp.minimum(members, row_total - 1)
        member_rows = unit_rows[safe_members].astype(jnp.float32)
        member_keys = jnp.where(members < row_total, row_keys[safe_members], -1).astype(jnp.int32)

        def per_block(block_number):
            start = (block_number * block_width).astype(jnp.int32)
            query_rows = lax.dynamic_slice_in_dim(member_rows, start, block_width, 0)
            query_keys = lax.dynamic_slice_in_dim(member_keys, start, block_width, 0)
            scores = jnp.dot(query_rows, member_rows.T, preferred_element_type=jnp.float32)
            cluster_base = query_keys // row_total * row_total
            allowed = (member_keys[None, :] >= cluster_base[:, None]) & (member_keys[None, :] < query_keys[:, None]) & (query_keys[:, None] >= 0)
            return lax.optimization_barrier(jnp.max(jnp.where(allowed, scores, jnp.float32(-1.0)), axis=1))
        found = lax.map(per_block, jnp.arange(group_width // block_width, dtype=jnp.int32)).reshape(-1)
        return (members, found)
    members, found = lax.map(per_group, jnp.arange(N_OWNER, dtype=jnp.int32))
    result = jnp.full((row_total,), -1.0, jnp.float32)
    return result.at[members.reshape(-1)].set(found.reshape(-1), mode='drop')
```

```python
import jax
import jax.numpy as jnp
from jax import lax
from jax.experimental import pallas as pl
from jax.experimental.pallas import tpu as pltpu
from jax.sharding import PartitionSpec as P

MESH = pl.DeviceIdType.MESH
NX, NY, NZ = 4, 8, 8
CAP = 14
SLOT = 16
NQ = NX
CHUNK = NZ * CAP
ROWS = 224
DIM = 1024
SPAN = 1 << 17
CLASSES = NX * NZ


def gray(v):
    return v ^ (v >> 1)


def eye(rows, lanes):
    return lax.broadcasted_iota(jnp.int32, (rows, lanes), 0) == lax.broadcasted_iota(
        jnp.int32, (rows, lanes), 1
    )


def column_of(row, rows):
    lanes = row.shape[1]
    zero = jnp.zeros((rows, lanes), row.dtype)
    spread = jnp.broadcast_to(row, (rows, lanes))
    return jnp.sum(jnp.where(eye(rows, lanes), spread, zero), axis=1, keepdims=True)


def contract_lanes(left, right):
    return lax.dot_general(
        left, right, (((1,), (1,)), ((), ())), preferred_element_type=jnp.float32
    )


def kernel(
    emb_ref, cid_ref, idx_ref, out_ref,
    unit, send, recv, held, query, keys, key_cols, clu_cols, scores, best_k, best_q,
    part_out, part_in, final, back,
    a2a_send, a2a_recv, y_send, y_recv, k_send, k_recv, p_send, p_recv, b_send, b_recv,
):
    owner = lax.axis_index("owner")
    panel = lax.axis_index("panel")
    x, zh, core = owner // 8, (owner // 2) % 4, owner % 2
    zl, y = panel // 8, panel % 8
    z = zh * 2 + zl

    def at(ax, ay, az, ac):
        return {"owner": (ax * 4 + az // 2) * 2 + ac, "panel": (az % 2) * 8 + ay}

    def along_y(step, ac):
        return at(x, (y + step + NY) % NY, z, ac)

    other = 1 - core
    ring = [along_y(s, core) for s in (-2, -1, 1, 2)] + [
        along_y(-2, other), along_y(0, other), along_y(2, other)
    ]

    barrier = pltpu.get_barrier_semaphore()

    def greet(k, carry):
        pl.semaphore_signal(
            barrier, inc=1, device_id=at((x + k // NZ) % NX, y, (z + k % NZ) % NZ, core),
            device_id_type=MESH,
        )
        return carry

    lax.fori_loop(1, CLASSES, greet, 0)
    for peer in ring:
        pl.semaphore_signal(barrier, inc=1, device_id=peer, device_id_type=MESH)

    wide = emb_ref[...].astype(jnp.float32)
    inverse = lax.rsqrt(jnp.sum(wide * wide, axis=1, keepdims=True) + 1e-06)
    unit[...] = (wide * inverse).astype(jnp.bfloat16)
    cid = cid_ref[...]
    residue = cid & (CLASSES - 1)
    quarter = gray(((residue >> 3) - x) & (NX - 1))
    offset = quarter * NZ + (((residue & 7) - z) & (NZ - 1))
    key = (cid >> 5) * SPAN + idx_ref[...] + 1
    offset_col = column_of(offset, ROWS)
    key_col = column_of(key, ROWS)
    first = lax.broadcasted_iota(jnp.int32, (ROWS, ROWS), 0)
    second = lax.broadcasted_iota(jnp.int32, (ROWS, ROWS), 1)
    equal = offset_col == offset
    rank = jnp.sum((equal & (first < second)).astype(jnp.int32), axis=0, keepdims=True)
    rank_col = jnp.sum((equal & (second < first)).astype(jnp.int32), axis=1, keepdims=True)
    lane = lax.broadcasted_iota(jnp.int32, (ROWS, 128), 1)
    digits = jnp.zeros((ROWS, 128), jnp.int32)
    for d, shift in enumerate((14, 7, 0)):
        digits = jnp.where(lane == SLOT * d + rank_col, (key_col >> shift) & 127, digits)
    digits = digits.astype(jnp.float32).astype(jnp.bfloat16)

    pl.semaphore_wait(barrier, CLASSES - 1 + len(ring))

    for q in range(NQ):
        slot = lax.broadcasted_iota(jnp.int32, (NZ * SLOT, ROWS), 0) + q * NZ * SLOT
        pick = (slot == offset * SLOT + rank).astype(jnp.float32).astype(jnp.bfloat16)
        pick_key = (slot == offset * SLOT + CAP).astype(jnp.float32).astype(jnp.bfloat16)
        rows = jnp.dot(pick, unit[...], preferred_element_type=jnp.float32)
        extra = jnp.dot(pick_key, digits, preferred_element_type=jnp.float32)
        base = q * NZ * SLOT
        send[base : base + NZ * SLOT, :] = rows.astype(jnp.bfloat16)
        send[base : base + NZ * SLOT, 0:128] = (rows[:, 0:128] + extra).astype(jnp.bfloat16)
        if q == 0:
            recv[0, 0:SLOT, :] = send[0:SLOT, :]

        def give(dz, carry, q=q, base=base):
            pltpu.make_async_remote_copy(
                src_ref=send.at[pl.ds(pl.multiple_of(base + dz * SLOT, SLOT), SLOT)],
                dst_ref=recv.at[q, pl.ds(pl.multiple_of(dz * SLOT, SLOT), SLOT)],
                send_sem=a2a_send,
                recv_sem=a2a_recv.at[q],
                device_id=at((x + gray(q)) % NX, y, (z + dz) % NZ, core),
                device_id_type=MESH,
            ).start()
            return carry

        lax.fori_loop(1 if q == 0 else 0, NZ, give, 0)

    def block(q, j):
        if j < 4:
            return held.at[q, pl.ds(j * CHUNK, CHUNK)]
        return query.at[q, pl.ds((j - 4) * 128, CHUNK)]

    def pass_on(q, j, peer, to):
        rows = pltpu.make_async_remote_copy(
            src_ref=block(q, j), dst_ref=block(q, to),
            send_sem=y_send.at[q, to], recv_sem=y_recv.at[q, to],
            device_id=peer, device_id_type=MESH,
        )
        names = pltpu.make_async_remote_copy(
            src_ref=keys.at[q, j], dst_ref=keys.at[q, to],
            send_sem=k_send.at[q, to], recv_sem=k_recv.at[q, to],
            device_id=peer, device_id_type=MESH,
        )
        rows.start()
        names.start()
        return rows, names

    copies = {}
    right, left = along_y(1, core), along_y(-1, core)

    def arrived(q, j):
        for copy in copies[q, j]:
            copy.wait_recv()

    slot_row = lax.broadcasted_iota(jnp.int32, (CHUNK, NZ * SLOT), 0)
    slot_col = lax.broadcasted_iota(jnp.int32, (CHUNK, NZ * SLOT), 1)
    source, place = slot_row // CAP, slot_row % CAP
    squeeze = (slot_col == source * SLOT + place).astype(jnp.float32).astype(jnp.bfloat16)
    key_rows = (slot_col == source * SLOT + CAP).astype(jnp.float32).astype(jnp.bfloat16)
    own_digit = (slot_col < 3 * SLOT) & (slot_col % SLOT == place)
    digit_sum = (
        lax.broadcasted_iota(jnp.int32, (8, 128), 1) // SLOT
        == lax.broadcasted_iota(jnp.int32, (8, 128), 0)
    ).astype(jnp.float32).astype(jnp.bfloat16)

    def own(q):
        if q == 0:
            landed = recv.at[0, pl.ds(SLOT, (NZ - 1) * SLOT)]
        else:
            landed = recv.at[q]
        pltpu.make_async_copy(landed, landed, a2a_recv.at[q]).wait()
        held[q, 2 * CHUNK : 3 * CHUNK, :] = jnp.dot(
            squeeze, recv[q], preferred_element_type=jnp.float32
        ).astype(jnp.bfloat16)
        spread = jnp.dot(key_rows, recv[q, :, 0:128], preferred_element_type=jnp.float32)
        spread = jnp.where(own_digit, spread, 0.0).astype(jnp.bfloat16)
        sums = contract_lanes(digit_sum, spread)
        value = sums[0:1] * 16384.0 + sums[1:2] * 128.0 + sums[2:3]
        keys[q, 2] = jnp.concatenate([value, jnp.zeros((1, 128 - CHUNK), jnp.float32)], axis=1)
        copies[q, 1] = pass_on(q, 2, right, 1)
        copies[q, 3] = pass_on(q, 2, left, 3)

    def forward(q):
        arrived(q, 1)
        copies[q, 0] = pass_on(q, 1, right, 0)
        arrived(q, 3)
        copies[q, 4] = pass_on(q, 3, left, 4)

    def far(q):
        arrived(q, 4)
        copies[q, 5] = pass_on(q, 4, along_y(0, other), 5)
        arrived(q, 0)

    def cluster_of(value):
        return jnp.floor((value - 1.0) * (1.0 / SPAN))

    def compare(q):
        arrived(q, 5)
        for j in range(5):
            column = column_of(keys[q, j], CHUNK)
            column = jnp.broadcast_to(column, (CHUNK, 128))
            key_cols[q, j * CHUNK : (j + 1) * CHUNK, :] = column
            clu_cols[q, j * CHUNK : (j + 1) * CHUNK, :] = cluster_of(column)

        def tile(t, carry):
            qk = jnp.where(t <= q, q, t - q - 1)
            qq = jnp.where(t <= q, t, q)
            right_rows = query[qq]
            scores[0 : 4 * CHUNK, :] = contract_lanes(held[qk], right_rows)
            scores[4 * CHUNK : 5 * CHUNK, :] = contract_lanes(query[qk, 0:CHUNK, :], right_rows)
            col_best = best_q[qq]
            halves = []
            for h in range(2):
                key_row = keys[qq, 4 + h]
                halves.append((key_row, cluster_of(key_row)))
            tops = [col_best[:, 0:128], col_best[:, 128:256]]
            for g in range(5 * CHUNK // 8):
                at_rows = pl.ds(g * 8, 8)
                key_col = key_cols[qk, at_rows, :]
                clu_col = clu_cols[qk, at_rows, :]
                top = best_k[qk, at_rows, :]
                for h in range(2):
                    key_row, clu_row = halves[h]
                    value = scores[at_rows, h * 128 : (h + 1) * 128]
                    value = jnp.where(clu_col == clu_row, value, -1.0)
                    top = jnp.maximum(top, jnp.where(key_row < key_col, value, -1.0))
                    tops[h] = jnp.maximum(tops[h], jnp.where(key_col < key_row, value, -1.0))
                best_k[qk, at_rows, :] = top
            best_q[qq, :, 0:128] = tops[0]
            best_q[qq, :, 128:256] = tops[1]
            return carry

        lax.fori_loop(0, 2 * q + 1, tile, 0)

    best_k[...] = jnp.full(best_k.shape, -1.0, jnp.float32)
    best_q[...] = jnp.full(best_q.shape, -1.0, jnp.float32)
    for q in range(NQ):
        for h in range(2):
            query[q, h * 128 + CHUNK : (h + 1) * 128, :] = jnp.zeros((128 - CHUNK, DIM), jnp.bfloat16)

    own(0)
    own(1)
    forward(0)
    own(2)
    forward(1)
    far(0)
    own(3)
    forward(2)
    far(1)
    compare(0)
    forward(3)
    far(2)
    compare(1)
    far(3)
    compare(2)
    compare(3)

    square = eye(CHUNK, 128)
    for q in range(NQ):
        for j in range(5):
            column = jnp.max(best_k[q, j * CHUNK : (j + 1) * CHUNK, :], axis=1, keepdims=True)
            row = jnp.max(
                jnp.where(square, jnp.broadcast_to(column, (CHUNK, 128)), -1.0), axis=0, keepdims=True
            )
            if j == 4:
                row = jnp.maximum(row, jnp.max(best_q[q, :, 0:128], axis=0, keepdims=True))
            part_out[j, q : q + 1, :] = row
        part_out[5, q : q + 1, :] = jnp.max(best_q[q, :, 128:256], axis=0, keepdims=True)
    parts = []
    for j, peer in (
        (0, along_y(-2, core)), (1, left), (3, right),
        (4, along_y(2, core)), (5, along_y(2, other)),
    ):
        part_out[j, 4:8, :] = jnp.full((4, 128), -1.0, jnp.float32)
        copy = pltpu.make_async_remote_copy(
            src_ref=part_out.at[j], dst_ref=part_in.at[j],
            send_sem=p_send.at[j], recv_sem=p_recv.at[j],
            device_id=peer, device_id_type=MESH,
        )
        copy.start()
        parts.append((j, copy))
    best = part_out[2, 0:NQ, :]
    for j, copy in parts:
        copy.wait_recv()
        best = jnp.maximum(best, part_in[j, 0:NQ, :])
    for q in range(NQ):
        final[q] = best[q : q + 1, :]
    back[0] = best[0:1, :]

    for q in range(NQ):

        def give_back(dz, carry, q=q):
            pltpu.make_async_remote_copy(
                src_ref=final.at[q],
                dst_ref=back.at[q * NZ + dz],
                send_sem=b_send,
                recv_sem=b_recv,
                device_id=at((x - gray(q) + NX) % NX, y, (z - dz + NZ) % NZ, core),
                device_id_type=MESH,
            ).start()
            return carry

        lax.fori_loop(1 if q == 0 else 0, NZ, give_back, 0)

    inbound = back.at[pl.ds(1, CLASSES - 1)]
    pltpu.make_async_copy(inbound, inbound, b_recv).wait()
    lane_row = lax.broadcasted_iota(jnp.int32, (1, 128), 1)
    spot = (offset & (NZ - 1)) * CAP + rank
    hit = lax.broadcasted_iota(jnp.int32, (128, ROWS), 0) == spot
    result = jnp.zeros((1, ROWS), jnp.float32)
    for q in range(NQ):
        mine = jnp.zeros((1, 128), jnp.float32)
        for dz in range(NZ):
            mine = jnp.where(lane_row // CAP == dz, back[q * NZ + dz], mine)
        column = jnp.broadcast_to(column_of(mine, 128), (128, ROWS))
        chosen = jnp.sum(jnp.where(hit, column, 0.0), axis=0, keepdims=True)
        result = jnp.where(offset >> 3 == q, chosen, result)
    out_ref[...] = result

    gone = send.at[pl.ds(SLOT, (CLASSES - 1) * SLOT)]
    pltpu.make_async_copy(gone, gone, a2a_send).wait()
    for pair in copies.values():
        for copy in pair:
            copy.wait_send()
    for j, copy in parts:
        copy.wait_send()
    pltpu.make_async_copy(inbound, inbound, b_send).wait()


def per_device(embeddings, cluster_id, row_index):
    vmem = pl.BlockSpec(memory_space=pltpu.VMEM)
    result = pl.pallas_call(
        kernel,
        out_shape=jax.ShapeDtypeStruct((1, ROWS), jnp.float32),
        in_specs=[vmem] * 3,
        out_specs=vmem,
        scratch_shapes=[
            pltpu.VMEM((ROWS, DIM), jnp.bfloat16),
            pltpu.VMEM((CLASSES * SLOT, DIM), jnp.bfloat16),
            pltpu.VMEM((NQ, NZ * SLOT, DIM), jnp.bfloat16),
            pltpu.VMEM((NQ, 4 * CHUNK, DIM), jnp.bfloat16),
            pltpu.VMEM((NQ, 256, DIM), jnp.bfloat16),
            pltpu.VMEM((NQ, 6, 1, 128), jnp.float32),
            pltpu.VMEM((NQ, 5 * CHUNK, 128), jnp.float32),
            pltpu.VMEM((NQ, 5 * CHUNK, 128), jnp.float32),
            pltpu.VMEM((5 * CHUNK, 256), jnp.float32),
            pltpu.VMEM((NQ, 5 * CHUNK, 128), jnp.float32),
            pltpu.VMEM((NQ, 8, 256), jnp.float32),
            pltpu.VMEM((6, 8, 128), jnp.float32),
            pltpu.VMEM((6, 8, 128), jnp.float32),
            pltpu.VMEM((NQ, 1, 128), jnp.float32),
            pltpu.VMEM((CLASSES, 1, 128), jnp.float32),
            pltpu.SemaphoreType.DMA,
            pltpu.SemaphoreType.DMA((NQ,)),
            pltpu.SemaphoreType.DMA((NQ, 6)),
            pltpu.SemaphoreType.DMA((NQ, 6)),
            pltpu.SemaphoreType.DMA((NQ, 6)),
            pltpu.SemaphoreType.DMA((NQ, 6)),
            pltpu.SemaphoreType.DMA((6,)),
            pltpu.SemaphoreType.DMA((6,)),
            pltpu.SemaphoreType.DMA,
            pltpu.SemaphoreType.DMA,
        ],
        compiler_params=pltpu.CompilerParams(
            collective_id=0, has_side_effects=True, vmem_limit_bytes=48 * 1024 * 1024
        ),
    )(embeddings, cluster_id.reshape(1, ROWS), row_index.reshape(1, ROWS))
    return result.reshape(ROWS)


def solution(mesh):
    placed = (P(("owner", "panel"), None), P(("owner", "panel")), P(("owner", "panel")))
    return jax.shard_map(
        per_device, mesh=mesh, in_specs=placed, out_specs=P(("owner", "panel")), check_vma=False
    )
```

```python
import jax
import jax.numpy as jnp
from jax import lax
from jax.experimental import pallas as pl
from jax.experimental.pallas import tpu as pltpu
from jax.sharding import PartitionSpec as P

MESH = pl.DeviceIdType.MESH
NX, NY, NZ = 4, 8, 8
CAP = 14
SLOT = 16
NQ = 4
PER = 8
CHUNK = PER * CAP
ROWS = 224
DIM = 1024
SPAN = 1 << 17
CLASSES = NQ * PER
HELD = 3 * CHUNK


def eye(rows, lanes):
    return lax.broadcasted_iota(jnp.int32, (rows, lanes), 0) == lax.broadcasted_iota(
        jnp.int32, (rows, lanes), 1
    )


def column_of(row, rows):
    lanes = row.shape[1]
    zero = jnp.zeros((rows, lanes), row.dtype)
    spread = jnp.broadcast_to(row, (rows, lanes))
    return jnp.sum(jnp.where(eye(rows, lanes), spread, zero), axis=1, keepdims=True)


def contract_lanes(left, right):
    return lax.dot_general(
        left, right, (((1,), (1,)), ((), ())), preferred_element_type=jnp.float32
    )


def to_bf16(mask):
    return mask.astype(jnp.float32).astype(jnp.bfloat16)


def y_steps(q, h):
    if q == 0:
        return 4 * h
    return q + h * (NY - 2 * q)


def kernel(
    emb_hbm, cid_hbm, idx_hbm, out_ref,
    emb_ref, cid_ref, idx_ref, unit, send, recv, held, query, keys, key_cols, clu_cols, scores,
    best_k, best_q, part_out, part_in, final, back,
    in_sem, a2a_send, a2a_recv, y_send, y_recv, k_send, k_recv, p_send, p_recv, b_send, b_recv,
):
    owner = lax.axis_index("owner")
    panel = lax.axis_index("panel")
    x, zh, core = owner // 8, (owner // 2) % 4, owner % 2
    zl, y = panel // 8, panel % 8
    z = zh * 2 + zl

    loads = [
        pltpu.make_async_copy(src, dst, in_sem.at[i])
        for i, (src, dst) in enumerate(
            ((cid_hbm, cid_ref), (idx_hbm, idx_ref), (emb_hbm, emb_ref))
        )
    ]
    for load in loads:
        load.start()

    def at(ax, ay, az, ac):
        return {"owner": (ax * 4 + az // 2) * 2 + ac, "panel": (az % 2) * 8 + ay}

    def along_x(step):
        return at((x + step + NX) % NX, y, z, core)

    def home(q, n):
        m = n % 4
        up = jnp.where((z + m) % 2 == 0, m, NZ - m)
        return at(x, (y + y_steps(q, n // 4)) % NY, (z + up) % NZ, core)

    def source(q, n):
        m = n % 4
        up = jnp.where(z % 2 == 0, NZ - m, m)
        return at(x, (y - y_steps(q, n // 4) + NY) % NY, (z + up) % NZ, core)

    pair_z = zh * 2 + 1 - zl
    pair, twin = at(x, y, pair_z, core), at(x, y, z, 1 - core)
    barrier = pltpu.get_barrier_semaphore()
    for q in range(NQ):

        def greet(n, carry, q=q):
            pl.semaphore_signal(barrier, inc=1, device_id=source(q, n), device_id_type=MESH)
            return carry

        lax.fori_loop(1 if q == 0 else 0, PER, greet, 0)
    nearby = [along_x(-1), along_x(1), pair, twin]
    for peer in nearby:
        pl.semaphore_signal(barrier, inc=1, device_id=peer, device_id_type=MESH)

    for load in loads[:2]:
        load.wait()
    cid = cid_ref[...]
    residue = cid & (CLASSES - 1)
    dy = ((residue >> 2) - y) & (NY - 1)
    quarter = jnp.where(dy == 4, 0, jnp.where(dy < 4, dy, NY - dy))
    half = (dy >= 4).astype(jnp.int32)
    dz = (z - 2 * (residue & 3)) & (NZ - 1)
    member = jnp.where((dz == 0) | (dz > 4), (NZ - dz) & (NZ - 1), dz - 1)
    place = half * 4 + member
    offset = quarter * PER + place
    key = (cid >> 5) * SPAN + idx_ref[...] + 1
    offset_col = column_of(offset, ROWS)
    key_col = column_of(key, ROWS)
    first = lax.broadcasted_iota(jnp.int32, (ROWS, ROWS), 0)
    second = lax.broadcasted_iota(jnp.int32, (ROWS, ROWS), 1)
    equal = offset_col == offset
    rank = jnp.sum((equal & (first < second)).astype(jnp.int32), axis=0, keepdims=True)
    rank_col = jnp.sum((equal & (second < first)).astype(jnp.int32), axis=1, keepdims=True)
    lane = lax.broadcasted_iota(jnp.int32, (ROWS, 128), 1)
    digits = jnp.zeros((ROWS, 128), jnp.int32)
    for d, shift in enumerate((14, 7, 0)):
        digits = jnp.where(lane == SLOT * d + rank_col, (key_col >> shift) & 127, digits)
    digits = digits.astype(jnp.float32).astype(jnp.bfloat16)

    loads[2].wait()
    wide = emb_ref[...].astype(jnp.float32)
    inverse = lax.rsqrt(jnp.sum(wide * wide, axis=1, keepdims=True) + 1e-06)
    unit[...] = (wide * inverse).astype(jnp.bfloat16)
    for q in range(NQ):
        base = q * PER * SLOT
        slot = lax.broadcasted_iota(jnp.int32, (PER * SLOT, ROWS), 0) + base
        pick = to_bf16(slot == offset * SLOT + rank)
        pick_key = to_bf16(slot == offset * SLOT + CAP)
        rows = jnp.dot(pick, unit[...], preferred_element_type=jnp.float32)
        extra = jnp.dot(pick_key, digits, preferred_element_type=jnp.float32)
        send[base : base + PER * SLOT, :] = rows.astype(jnp.bfloat16)
        send[base : base + PER * SLOT, 0:128] = (rows[:, 0:128] + extra).astype(jnp.bfloat16)
    recv[0, 0:SLOT, :] = send[0:SLOT, :]
    best_k[...] = jnp.full(best_k.shape, -1.0, jnp.float32)
    best_q[...] = jnp.full(best_q.shape, -1.0, jnp.float32)
    for q in range(NQ):
        for u in range(4):
            query[q, u * 128 + CHUNK : (u + 1) * 128, :] = jnp.zeros(
                (128 - CHUNK, DIM), jnp.bfloat16
            )

    pl.semaphore_wait(barrier, CLASSES - 1 + len(nearby))

    for q in range(NQ):

        def give(n, carry, q=q):
            start = pl.multiple_of(n * SLOT, SLOT)
            pltpu.make_async_remote_copy(
                src_ref=send.at[pl.ds(q * PER * SLOT + start, SLOT)],
                dst_ref=recv.at[q, pl.ds(start, SLOT)],
                send_sem=a2a_send,
                recv_sem=a2a_recv.at[q],
                device_id=home(q, n),
                device_id_type=MESH,
            ).start()
            return carry

        lax.fori_loop(1 if q == 0 else 0, PER, give, 0)

    def block(q, j):
        if j < 2:
            return held.at[q, pl.ds(j * CHUNK, CHUNK)]
        return query.at[q, pl.ds((j - 2) * 128, CHUNK)]

    copies = {}

    def pass_on(q, j, peer, to):
        rows = pltpu.make_async_remote_copy(
            src_ref=block(q, j), dst_ref=block(q, to),
            send_sem=y_send.at[q, to], recv_sem=y_recv.at[q, to],
            device_id=peer, device_id_type=MESH,
        )
        names = pltpu.make_async_remote_copy(
            src_ref=keys.at[q, j], dst_ref=keys.at[q, to],
            send_sem=k_send.at[q, to], recv_sem=k_recv.at[q, to],
            device_id=peer, device_id_type=MESH,
        )
        rows.start()
        names.start()
        copies[q, to] = rows, names

    def arrived(q, j):
        for copy in copies[q, j]:
            copy.wait_recv()

    slot_row = lax.broadcasted_iota(jnp.int32, (CHUNK, PER * SLOT), 0)
    slot_col = lax.broadcasted_iota(jnp.int32, (CHUNK, PER * SLOT), 1)
    sender, nth = slot_row // CAP, slot_row % CAP
    squeeze = to_bf16(slot_col == sender * SLOT + nth)
    key_rows = to_bf16(slot_col == sender * SLOT + CAP)
    own_digit = (slot_col < 3 * SLOT) & (slot_col % SLOT == nth)
    digit_sum = to_bf16(
        lax.broadcasted_iota(jnp.int32, (8, 128), 1) // SLOT
        == lax.broadcasted_iota(jnp.int32, (8, 128), 0)
    )

    def own(q):
        landed = recv.at[0, pl.ds(SLOT, (PER - 1) * SLOT)] if q == 0 else recv.at[q]
        pltpu.make_async_copy(landed, landed, a2a_recv.at[q]).wait()
        held[q, CHUNK : 2 * CHUNK, :] = jnp.dot(
            squeeze, recv[q], preferred_element_type=jnp.float32
        ).astype(jnp.bfloat16)
        spread = jnp.dot(key_rows, recv[q, :, 0:128], preferred_element_type=jnp.float32)
        spread = jnp.where(own_digit, spread, 0.0).astype(jnp.bfloat16)
        sums = contract_lanes(digit_sum, spread)
        value = sums[0:1] * 16384.0 + sums[1:2] * 128.0 + sums[2:3]
        keys[q, 1] = jnp.concatenate([value, jnp.zeros((1, 128 - CHUNK), jnp.float32)], axis=1)
        pass_on(q, 1, along_x(-1), 2)
        pass_on(q, 1, along_x(1), 0)

    def cross(q):
        arrived(q, 2)
        pass_on(q, 2, pair, 3)
        pass_on(q, 2, twin, 4)

    def share(q):
        arrived(q, 3)
        pass_on(q, 3, twin, 5)

    def cluster_of(value):
        return jnp.floor((value - 1.0) * (1.0 / SPAN))

    def near(q):
        arrived(q, 0)
        for j in range(3):
            column = jnp.broadcast_to(column_of(keys[q, j], CHUNK), (CHUNK, 128))
            key_cols[q, j * CHUNK : (j + 1) * CHUNK, :] = column
            clu_cols[q, j * CHUNK : (j + 1) * CHUNK, :] = cluster_of(column)

    def far(q):
        arrived(q, 4)
        arrived(q, 5)

    def tile(qk, qq):
        right_rows = query[qq]
        scores[0 : 2 * CHUNK, :] = contract_lanes(held[qk], right_rows)
        scores[2 * CHUNK : HELD, :] = contract_lanes(query[qk, 0:CHUNK, :], right_rows)
        key_row = [keys[qq, 2 + u] for u in range(4)]
        clu_row = [cluster_of(row) for row in key_row]
        tops = [best_q[qq, :, u * 128 : (u + 1) * 128] for u in range(4)]
        for g in range(HELD // 8):
            at_rows = slice(g * 8, g * 8 + 8)
            key_here = key_cols[qk, at_rows, :]
            clu_here = clu_cols[qk, at_rows, :]
            top = best_k[qk, at_rows, :]
            for u in range(4):
                value = scores[at_rows, u * 128 : (u + 1) * 128]
                value = jnp.where(clu_here == clu_row[u], value, -1.0)
                top = jnp.maximum(top, jnp.where(key_row[u] < key_here, value, -1.0))
                if CHUNK <= g * 8 < 2 * CHUNK:
                    tops[u] = jnp.maximum(tops[u], jnp.where(key_here < key_row[u], value, -1.0))
            best_k[qk, at_rows, :] = top
        for u in range(4):
            best_q[qq, :, u * 128 : (u + 1) * 128] = tops[u]

    def tiles(count, pick):
        def step(t, carry):
            tile(*pick(t))
            return carry

        lax.fori_loop(0, count, step, 0)

    def both_ways(q):
        return lambda t: (jnp.where(t <= q, q, t - q - 1), jnp.where(t <= q, t, q))

    own(0)
    own(1)
    cross(0)
    own(2)
    cross(1)
    share(0)
    near(0)
    cross(2)
    own(3)
    share(1)
    near(1)
    far(0)
    tiles(1, both_ways(0))
    share(2)
    far(1)
    tiles(3, both_ways(1))
    cross(3)
    near(2)
    far(2)
    near(3)
    tiles(5, both_ways(2))
    tiles(3, lambda t: (3, t))
    share(3)
    far(3)
    tiles(4, lambda t: (t, 3))

    square = eye(CHUNK, 128)

    def over_query(q, j):
        column = jnp.max(best_k[q, j * CHUNK : (j + 1) * CHUNK, :], axis=1, keepdims=True)
        column = jnp.broadcast_to(column, (CHUNK, 128))
        return jnp.max(jnp.where(square, column, -1.0), axis=0, keepdims=True)

    for q in range(NQ):
        for u in range(4):
            row = jnp.max(best_q[q, :, u * 128 : (u + 1) * 128], axis=0, keepdims=True)
            if u == 0:
                row = jnp.maximum(row, over_query(q, 2))
            part_out[u, q : q + 1, :] = row
        part_out[4, q : q + 1, :] = over_query(q, 0)
    parts = []
    ahead = (x + 1) % NX
    for u, peer in enumerate((
        at(ahead, y, z, core), at(ahead, y, pair_z, core),
        at(ahead, y, z, 1 - core), at(ahead, y, pair_z, 1 - core), along_x(-1),
    )):
        part_out[u, NQ:8, :] = jnp.full((8 - NQ, 128), -1.0, jnp.float32)
        copy = pltpu.make_async_remote_copy(
            src_ref=part_out.at[u], dst_ref=part_in.at[u],
            send_sem=p_send.at[u], recv_sem=p_recv.at[u],
            device_id=peer, device_id_type=MESH,
        )
        copy.start()
        parts.append(copy)
    best = [over_query(q, 1) for q in range(NQ)]
    for u, copy in enumerate(parts):
        copy.wait_recv()
        best = [jnp.maximum(best[q], part_in[u, q : q + 1, :]) for q in range(NQ)]
    for q in range(NQ):
        final[q] = best[q]
    back[0] = best[0]

    for q in range(NQ):

        def give_back(n, carry, q=q):
            pltpu.make_async_remote_copy(
                src_ref=final.at[q],
                dst_ref=back.at[q * PER + n],
                send_sem=b_send,
                recv_sem=b_recv,
                device_id=source(q, n),
                device_id_type=MESH,
            ).start()
            return carry

        lax.fori_loop(1 if q == 0 else 0, PER, give_back, 0)

    inbound = back.at[pl.ds(1, CLASSES - 1)]
    pltpu.make_async_copy(inbound, inbound, b_recv).wait()
    lane_row = lax.broadcasted_iota(jnp.int32, (1, 128), 1)
    hit = lax.broadcasted_iota(jnp.int32, (128, ROWS), 0) == place * CAP + rank
    result = jnp.zeros((1, ROWS), jnp.float32)
    for q in range(NQ):
        mine = jnp.zeros((1, 128), jnp.float32)
        for n in range(PER):
            mine = jnp.where(lane_row // CAP == n, back[q * PER + n], mine)
        column = jnp.broadcast_to(column_of(mine, 128), (128, ROWS))
        chosen = jnp.sum(jnp.where(hit, column, 0.0), axis=0, keepdims=True)
        result = jnp.where(quarter == q, chosen, result)
    out_ref[...] = result

    gone = send.at[pl.ds(SLOT, (CLASSES - 1) * SLOT)]
    pltpu.make_async_copy(gone, gone, a2a_send).wait()
    for both in copies.values():
        for copy in both:
            copy.wait_send()
    for copy in parts:
        copy.wait_send()
    pltpu.make_async_copy(inbound, inbound, b_send).wait()


def per_device(embeddings, cluster_id, row_index):
    result = pl.pallas_call(
        kernel,
        out_shape=jax.ShapeDtypeStruct((1, ROWS), jnp.float32),
        in_specs=[pl.BlockSpec(memory_space=pl.ANY)] * 3,
        out_specs=pl.BlockSpec(memory_space=pltpu.VMEM),
        scratch_shapes=[
            pltpu.VMEM((ROWS, DIM), jnp.bfloat16),
            pltpu.VMEM((1, ROWS), jnp.int32),
            pltpu.VMEM((1, ROWS), jnp.int32),
            pltpu.VMEM((ROWS, DIM), jnp.bfloat16),
            pltpu.VMEM((CLASSES * SLOT, DIM), jnp.bfloat16),
            pltpu.VMEM((NQ, PER * SLOT, DIM), jnp.bfloat16),
            pltpu.VMEM((NQ, 2 * CHUNK, DIM), jnp.bfloat16),
            pltpu.VMEM((NQ, 512, DIM), jnp.bfloat16),
            pltpu.VMEM((NQ, 6, 1, 128), jnp.float32),
            pltpu.VMEM((NQ, HELD, 128), jnp.float32),
            pltpu.VMEM((NQ, HELD, 128), jnp.float32),
            pltpu.VMEM((HELD, 512), jnp.float32),
            pltpu.VMEM((NQ, HELD, 128), jnp.float32),
            pltpu.VMEM((NQ, 8, 512), jnp.float32),
            pltpu.VMEM((5, 8, 128), jnp.float32),
            pltpu.VMEM((5, 8, 128), jnp.float32),
            pltpu.VMEM((NQ, 1, 128), jnp.float32),
            pltpu.VMEM((CLASSES, 1, 128), jnp.float32),
            pltpu.SemaphoreType.DMA((3,)),
            pltpu.SemaphoreType.DMA,
            pltpu.SemaphoreType.DMA((NQ,)),
            pltpu.SemaphoreType.DMA((NQ, 6)),
            pltpu.SemaphoreType.DMA((NQ, 6)),
            pltpu.SemaphoreType.DMA((NQ, 6)),
            pltpu.SemaphoreType.DMA((NQ, 6)),
            pltpu.SemaphoreType.DMA((5,)),
            pltpu.SemaphoreType.DMA((5,)),
            pltpu.SemaphoreType.DMA,
            pltpu.SemaphoreType.DMA,
        ],
        compiler_params=pltpu.CompilerParams(
            collective_id=0, has_side_effects=True, vmem_limit_bytes=48 * 1024 * 1024
        ),
    )(embeddings, cluster_id.reshape(1, ROWS), row_index.reshape(1, ROWS))
    return result.reshape(ROWS)


def solution(mesh):
    placed = (P(("owner", "panel"), None), P(("owner", "panel")), P(("owner", "panel")))
    return jax.shard_map(
        per_device, mesh=mesh, in_specs=placed, out_specs=P(("owner", "panel")), check_vma=False
    )
```

```python
import jax
import jax.numpy as jnp
from jax import lax
from jax.experimental import pallas as pl
from jax.experimental.pallas import tpu as pltpu
from jax.sharding import PartitionSpec as P

MESH = pl.DeviceIdType.MESH
NX, NY, NZ = 4, 8, 8
CAP = 14
SLOT = 16
NQ = 4
PER = 8
CHUNK = PER * CAP
ROWS = 224
DIM = 1024
SPAN = 1 << 17
CLASSES = NQ * PER
HELD = 3 * CHUNK


def eye(rows, lanes):
    return lax.broadcasted_iota(jnp.int32, (rows, lanes), 0) == lax.broadcasted_iota(
        jnp.int32, (rows, lanes), 1
    )


def column_of(row, rows):
    lanes = row.shape[1]
    zero = jnp.zeros((rows, lanes), row.dtype)
    spread = jnp.broadcast_to(row, (rows, lanes))
    return jnp.sum(jnp.where(eye(rows, lanes), spread, zero), axis=1, keepdims=True)


def contract_lanes(left, right):
    return lax.dot_general(
        left, right, (((1,), (1,)), ((), ())), preferred_element_type=jnp.float32
    )


def to_bf16(mask):
    return mask.astype(jnp.float32).astype(jnp.bfloat16)


def y_steps(n):
    return (n + 1) // 2 if n % 2 else (NY - n // 2) % NY


def z_steps(q):
    return (4 - q) % 4


FIRST = 48
FARTHEST = sorted(
    ((q, n) for q in range(NQ) for n in range(PER) if q or n),
    key=lambda slot: -(z_steps(slot[0]) + (slot[1] + 1) // 2),
)


def kernel(
    emb_hbm, cid_hbm, idx_hbm, out_ref,
    emb_ref, cid_ref, idx_ref, unit, send, recv, held, query, keys, key_cols, clu_cols, scores,
    best_k, best_q, part_out, part_in, final, back,
    in_sem, own_sem, a2a_send, a2a_recv, y_send, y_recv, k_send, k_recv, p_send, p_recv, b_send, b_recv,
):
    owner = lax.axis_index("owner")
    panel = lax.axis_index("panel")
    x, zh, core = owner // 8, (owner // 2) % 4, owner % 2
    zl, y = panel // 8, panel % 8
    z = zh * 2 + zl

    loads = [
        pltpu.make_async_copy(src, dst, in_sem.at[i])
        for i, (src, dst) in enumerate(
            ((cid_hbm, cid_ref), (idx_hbm, idx_ref), (emb_hbm, emb_ref))
        )
    ]
    for load in loads:
        load.start()

    def at(ax, ay, az, ac):
        return {"owner": (ax * 4 + az // 2) * 2 + ac, "panel": (az % 2) * 8 + ay}

    def along_x(step):
        return at((x + step + NX) % NX, y, z, core)

    def home(q, n):
        m = z_steps(q)
        up = jnp.where((z + m) % 2 == 0, m, NZ - m)
        return at(x, (y + y_steps(n)) % NY, (z + up) % NZ, core)

    def source(q, n):
        m = z_steps(q)
        up = jnp.where(z % 2 == 0, NZ - m, m)
        return at(x, (y - y_steps(n) + NY) % NY, (z + up) % NZ, core)

    pair_z = zh * 2 + 1 - zl
    pair, twin = at(x, y, pair_z, core), at(x, y, z, 1 - core)
    barrier = pltpu.get_barrier_semaphore()
    for q, n in FARTHEST:
        pl.semaphore_signal(barrier, inc=1, device_id=source(q, n), device_id_type=MESH)
    nearby = [along_x(-1), along_x(1), pair, twin]
    for peer in nearby:
        pl.semaphore_signal(barrier, inc=1, device_id=peer, device_id_type=MESH)

    for load in loads[:2]:
        load.wait()
    cid = cid_ref[...]
    residue = cid & (CLASSES - 1)
    dy = ((residue >> 2) - y) & (NY - 1)
    dz = (z - 2 * (residue & 3)) & (NZ - 1)
    member = jnp.where((dz == 0) | (dz > 4), (NZ - dz) & (NZ - 1), dz - 1)
    quarter = (4 - member) & 3
    place = jnp.where(dy <= 4, jnp.maximum(2 * dy - 1, 0), 2 * (NY - dy))
    offset = quarter * PER + place
    key = (cid >> 5) * SPAN + idx_ref[...] + 1
    offset_col = column_of(offset, ROWS)
    key_col = column_of(key, ROWS)
    first = lax.broadcasted_iota(jnp.int32, (ROWS, ROWS), 0)
    second = lax.broadcasted_iota(jnp.int32, (ROWS, ROWS), 1)
    equal = offset_col == offset
    rank = jnp.sum((equal & (first < second)).astype(jnp.int32), axis=0, keepdims=True)
    rank_col = jnp.sum((equal & (second < first)).astype(jnp.int32), axis=1, keepdims=True)
    lane = lax.broadcasted_iota(jnp.int32, (ROWS, 128), 1)
    digits = jnp.zeros((ROWS, 128), jnp.int32)
    for d, shift in enumerate((14, 7, 0)):
        digits = jnp.where(lane == SLOT * d + rank_col, (key_col >> shift) & 127, digits)
    digits = digits.astype(jnp.float32).astype(jnp.bfloat16)

    loads[2].wait()
    wide = emb_ref[...].astype(jnp.float32)
    inverse = lax.rsqrt(jnp.sum(wide * wide, axis=1, keepdims=True) + 1e-06)
    unit[...] = (wide * inverse).astype(jnp.bfloat16)
    for q in range(NQ):
        base = q * PER * SLOT
        slot = lax.broadcasted_iota(jnp.int32, (PER * SLOT, ROWS), 0) + base
        pick = to_bf16(slot == offset * SLOT + rank)
        pick_key = to_bf16(slot == offset * SLOT + CAP)
        rows = jnp.dot(pick, unit[...], preferred_element_type=jnp.float32)
        extra = jnp.dot(pick_key, digits, preferred_element_type=jnp.float32)
        send[base : base + PER * SLOT, :] = rows.astype(jnp.bfloat16)
        send[base : base + PER * SLOT, 0:128] = (rows[:, 0:128] + extra).astype(jnp.bfloat16)
    recv[0, 0:SLOT, :] = send[0:SLOT, :]
    best_k[...] = jnp.full(best_k.shape, -1.0, jnp.float32)
    best_q[...] = jnp.full(best_q.shape, -1.0, jnp.float32)
    for q in range(NQ):
        for s in range(2):
            for base in (CHUNK, 128 + CHUNK):
                query[q, s, base : base + 128 - CHUNK, :] = jnp.zeros(
                    (128 - CHUNK, DIM), jnp.bfloat16
                )

    pl.semaphore_wait(barrier, CLASSES - 1 + len(nearby))

    for q in range(NQ):
        for n in range(PER):
            if q or n:
                pltpu.make_async_remote_copy(
                    src_ref=send.at[pl.ds((q * PER + n) * SLOT, SLOT)],
                    dst_ref=recv.at[q, pl.ds(n * SLOT, SLOT)],
                    send_sem=a2a_send,
                    recv_sem=a2a_recv.at[q, n // 4],
                    device_id=home(q, n),
                    device_id_type=MESH,
                ).start()

    def part_of(q, j, h):
        start, size = (FIRST, CHUNK - FIRST) if h else (0, FIRST)
        if j < 2:
            return held.at[pl.ds(q * HELD + j * CHUNK + start, size)]
        return query.at[q, (j - 2) // 2, pl.ds((j - 2) % 2 * 128 + start, size)]

    copies = {}

    def pass_on(q, j, h, peer, to):
        copy = pltpu.make_async_remote_copy(
            src_ref=part_of(q, j, h), dst_ref=part_of(q, to, h),
            send_sem=y_send.at[q, to, h], recv_sem=y_recv.at[q, to, h],
            device_id=peer, device_id_type=MESH,
        )
        copy.start()
        copies[q, to, h] = copy
        if h:
            names = pltpu.make_async_remote_copy(
                src_ref=keys.at[q, j], dst_ref=keys.at[q, to],
                send_sem=k_send.at[q, to], recv_sem=k_recv.at[q, to],
                device_id=peer, device_id_type=MESH,
            )
            names.start()
            copies[q, to, 2] = names

    def arrived(q, j, h):
        copies[q, j, h].wait_recv()
        if h:
            copies[q, j, 2].wait_recv()

    def squeezer(start, size, below, width, nth=None):
        row = lax.broadcasted_iota(jnp.int32, (size, width), 0) + start
        col = lax.broadcasted_iota(jnp.int32, (size, width), 1) + below
        return to_bf16(col == row // CAP * SLOT + (row % CAP if nth is None else nth))

    squeeze = (
        squeezer(0, FIRST, 0, 4 * SLOT),
        squeezer(FIRST, CHUNK - FIRST, FIRST, PER * SLOT - FIRST),
    )
    key_rows = squeezer(0, CHUNK, 0, PER * SLOT, CAP)
    slot_col = lax.broadcasted_iota(jnp.int32, (CHUNK, PER * SLOT), 1)
    nth = lax.broadcasted_iota(jnp.int32, (CHUNK, PER * SLOT), 0) % CAP
    own_digit = (slot_col < 3 * SLOT) & (slot_col % SLOT == nth)
    digit_sum = to_bf16(
        lax.broadcasted_iota(jnp.int32, (8, 128), 1) // SLOT
        == lax.broadcasted_iota(jnp.int32, (8, 128), 0)
    )

    def own(q, h):
        skip = SLOT if q == 0 and h == 0 else 0
        landed = recv.at[q, pl.ds(h * 4 * SLOT + skip, 4 * SLOT - skip)]
        pltpu.make_async_copy(landed, landed, a2a_recv.at[q, h]).wait()
        base = q * HELD + CHUNK
        if h == 0:
            held[base : base + FIRST, :] = jnp.dot(
                squeeze[0], recv[q, 0 : 4 * SLOT, :], preferred_element_type=jnp.float32
            ).astype(jnp.bfloat16)
        else:
            held[base + FIRST : base + CHUNK, :] = jnp.dot(
                squeeze[1], recv[q, FIRST:, :], preferred_element_type=jnp.float32
            ).astype(jnp.bfloat16)
            spread = jnp.dot(key_rows, recv[q, :, 0:128], preferred_element_type=jnp.float32)
            spread = jnp.where(own_digit, spread, 0.0).astype(jnp.bfloat16)
            sums = contract_lanes(digit_sum, spread)
            value = sums[0:1] * 16384.0 + sums[1:2] * 128.0 + sums[2:3]
            keys[q, 1] = jnp.concatenate(
                [value, jnp.zeros((1, 128 - CHUNK), jnp.float32)], axis=1
            )
        pass_on(q, 1, h, along_x(-1), 2)
        pass_on(q, 1, h, along_x(1), 0)

    def own_copy(q, h):
        start, size = (FIRST, CHUNK - FIRST) if h else (0, FIRST)
        return pltpu.make_async_copy(
            part_of(q, 2, h),
            held.at[pl.ds(q * HELD + 2 * CHUNK + start, size)],
            own_sem.at[q, h],
        )

    def cross(q, h):
        arrived(q, 2, h)
        pass_on(q, 2, h, pair, 4)
        pass_on(q, 2, h, twin, 3)
        own_copy(q, h).start()

    def share(q, h):
        arrived(q, 4, h)
        pass_on(q, 4, h, twin, 5)

    def cluster_of(value):
        return jnp.floor((value - 1.0) * (1.0 / SPAN))

    def near(q):
        for h in range(2):
            arrived(q, 0, h)
            own_copy(q, h).wait()
        for j in range(3):
            column = jnp.broadcast_to(column_of(keys[q, j], CHUNK), (CHUNK, 128))
            base = q * HELD + j * CHUNK
            key_cols[base : base + CHUNK, :] = column
            clu_cols[base : base + CHUNK, :] = cluster_of(column)
        for h in range(2):
            arrived(q, 3, h)

    def far(q):
        for h in range(2):
            arrived(q, 5, h)

    def score(qk, qq, s):
        base = pl.multiple_of(qk * HELD, 16)
        scores[...] = contract_lanes(held[pl.ds(base, HELD), :], query[qq, s])
        key_row = [keys[qq, 2 + 2 * s + i] for i in range(2)]
        clu_row = [cluster_of(row) for row in key_row]
        tops = [best_q[qq, s, :, i * 128 : (i + 1) * 128] for i in range(2)]
        for g in range(HELD // 8):
            at_rows = pl.ds(pl.multiple_of(base + g * 8, 8), 8)
            key_here = key_cols[at_rows, :]
            clu_here = clu_cols[at_rows, :]
            top = best_k[at_rows, :]
            for i in range(2):
                value = scores[g * 8 : g * 8 + 8, i * 128 : (i + 1) * 128]
                value = jnp.where(clu_here == clu_row[i], value, -1.0)
                top = jnp.maximum(top, jnp.where(key_row[i] < key_here, value, -1.0))
                if CHUNK <= g * 8 < 2 * CHUNK:
                    tops[i] = jnp.maximum(tops[i], jnp.where(key_here < key_row[i], value, -1.0))
            best_k[at_rows, :] = top
        for i in range(2):
            best_q[qq, s, :, i * 128 : (i + 1) * 128] = tops[i]

    def score_all(count, pick):
        def step(t, carry):
            score(*pick(t))
            return carry

        lax.fori_loop(0, count, step, 0)

    def both_ways(q):
        def pick(t):
            k, s = t // 2, t % 2
            return jnp.where(k <= q, q, k - q - 1), jnp.where(k <= q, k, q), s

        return pick

    own(0, 0)
    own(0, 1)
    cross(0, 0)
    own(1, 0)
    cross(0, 1)
    own(1, 1)
    share(0, 0)
    own(2, 0)
    cross(1, 0)
    share(0, 1)
    cross(1, 1)
    own(2, 1)
    near(0)
    own(3, 0)
    cross(2, 0)
    share(1, 0)
    far(0)
    score_all(2, both_ways(0))
    own(3, 1)
    cross(2, 1)
    share(1, 1)
    near(1)
    far(1)
    share(2, 0)
    cross(3, 0)
    score_all(6, both_ways(1))
    cross(3, 1)
    share(2, 1)
    near(2)
    far(2)
    score_all(10, both_ways(2))
    share(3, 0)
    near(3)
    score_all(10, lambda t: (
        jnp.where(t < 6, 3, t - 6), jnp.where(t < 6, t // 2, 3), jnp.where(t < 6, t % 2, 0)
    ))
    share(3, 1)
    far(3)
    score_all(4, lambda t: (t, 3, 1))

    square = eye(CHUNK, 128)

    def over_query(q, j):
        base = q * HELD + j * CHUNK
        column = jnp.max(best_k[base : base + CHUNK, :], axis=1, keepdims=True)
        column = jnp.broadcast_to(column, (CHUNK, 128))
        return jnp.max(jnp.where(square, column, -1.0), axis=0, keepdims=True)

    for q in range(NQ):
        for u in range(4):
            lanes = slice(u % 2 * 128, u % 2 * 128 + 128)
            row = jnp.max(best_q[q, u // 2, :, lanes], axis=0, keepdims=True)
            if u == 0:
                row = jnp.maximum(row, over_query(q, 2))
            part_out[u, q : q + 1, :] = row
        part_out[4, q : q + 1, :] = over_query(q, 0)
    parts = []
    ahead = (x + 1) % NX
    for u, peer in enumerate((
        at(ahead, y, z, core), at(ahead, y, z, 1 - core),
        at(ahead, y, pair_z, core), at(ahead, y, pair_z, 1 - core), along_x(-1),
    )):
        part_out[u, NQ:8, :] = jnp.full((8 - NQ, 128), -1.0, jnp.float32)
        copy = pltpu.make_async_remote_copy(
            src_ref=part_out.at[u], dst_ref=part_in.at[u],
            send_sem=p_send.at[u], recv_sem=p_recv.at[u],
            device_id=peer, device_id_type=MESH,
        )
        copy.start()
        parts.append(copy)
    best = [over_query(q, 1) for q in range(NQ)]
    for u, copy in enumerate(parts):
        copy.wait_recv()
        best = [jnp.maximum(best[q], part_in[u, q : q + 1, :]) for q in range(NQ)]
    for q in range(NQ):
        final[q] = best[q]
    back[0] = best[0]

    for q, n in FARTHEST:
        pltpu.make_async_remote_copy(
            src_ref=final.at[q],
            dst_ref=back.at[q * PER + n],
            send_sem=b_send,
            recv_sem=b_recv,
            device_id=source(q, n),
            device_id_type=MESH,
        ).start()

    inbound = back.at[pl.ds(1, CLASSES - 1)]
    pltpu.make_async_copy(inbound, inbound, b_recv).wait()
    lane_row = lax.broadcasted_iota(jnp.int32, (1, 128), 1)
    hit = lax.broadcasted_iota(jnp.int32, (128, ROWS), 0) == place * CAP + rank
    result = jnp.zeros((1, ROWS), jnp.float32)
    for q in range(NQ):
        mine = jnp.zeros((1, 128), jnp.float32)
        for n in range(PER):
            mine = jnp.where(lane_row // CAP == n, back[q * PER + n], mine)
        column = jnp.broadcast_to(column_of(mine, 128), (128, ROWS))
        chosen = jnp.sum(jnp.where(hit, column, 0.0), axis=0, keepdims=True)
        result = jnp.where(quarter == q, chosen, result)
    out_ref[...] = result

    gone = send.at[pl.ds(SLOT, (CLASSES - 1) * SLOT)]
    pltpu.make_async_copy(gone, gone, a2a_send).wait()
    for copy in copies.values():
        copy.wait_send()
    for copy in parts:
        copy.wait_send()
    pltpu.make_async_copy(inbound, inbound, b_send).wait()


def per_device(embeddings, cluster_id, row_index):
    result = pl.pallas_call(
        kernel,
        out_shape=jax.ShapeDtypeStruct((1, ROWS), jnp.float32),
        in_specs=[pl.BlockSpec(memory_space=pl.ANY)] * 3,
        out_specs=pl.BlockSpec(memory_space=pltpu.VMEM),
        scratch_shapes=[
            pltpu.VMEM((ROWS, DIM), jnp.bfloat16),
            pltpu.VMEM((1, ROWS), jnp.int32),
            pltpu.VMEM((1, ROWS), jnp.int32),
            pltpu.VMEM((ROWS, DIM), jnp.bfloat16),
            pltpu.VMEM((CLASSES * SLOT, DIM), jnp.bfloat16),
            pltpu.VMEM((NQ, PER * SLOT, DIM), jnp.bfloat16),
            pltpu.VMEM((NQ * HELD, DIM), jnp.bfloat16),
            pltpu.VMEM((NQ, 2, 256, DIM), jnp.bfloat16),
            pltpu.VMEM((NQ, 6, 1, 128), jnp.float32),
            pltpu.VMEM((NQ * HELD, 128), jnp.float32),
            pltpu.VMEM((NQ * HELD, 128), jnp.float32),
            pltpu.VMEM((HELD, 256), jnp.float32),
            pltpu.VMEM((NQ * HELD, 128), jnp.float32),
            pltpu.VMEM((NQ, 2, 8, 256), jnp.float32),
            pltpu.VMEM((5, 8, 128), jnp.float32),
            pltpu.VMEM((5, 8, 128), jnp.float32),
            pltpu.VMEM((NQ, 1, 128), jnp.float32),
            pltpu.VMEM((CLASSES, 1, 128), jnp.float32),
            pltpu.SemaphoreType.DMA((3,)),
            pltpu.SemaphoreType.DMA((NQ, 2)),
            pltpu.SemaphoreType.DMA,
            pltpu.SemaphoreType.DMA((NQ, 2)),
            pltpu.SemaphoreType.DMA((NQ, 6, 2)),
            pltpu.SemaphoreType.DMA((NQ, 6, 2)),
            pltpu.SemaphoreType.DMA((NQ, 6)),
            pltpu.SemaphoreType.DMA((NQ, 6)),
            pltpu.SemaphoreType.DMA((5,)),
            pltpu.SemaphoreType.DMA((5,)),
            pltpu.SemaphoreType.DMA,
            pltpu.SemaphoreType.DMA,
        ],
        compiler_params=pltpu.CompilerParams(
            collective_id=0, has_side_effects=True, vmem_limit_bytes=62 * 1024 * 1024
        ),
    )(embeddings, cluster_id.reshape(1, ROWS), row_index.reshape(1, ROWS))
    return result.reshape(ROWS)


def solution(mesh):
    placed = (P(("owner", "panel"), None), P(("owner", "panel")), P(("owner", "panel")))
    return jax.shard_map(
        per_device, mesh=mesh, in_specs=placed, out_specs=P(("owner", "panel")), check_vma=False
    )
```

```python
import jax
import jax.numpy as jnp
from jax import lax
from jax.experimental import pallas as pl
from jax.experimental.pallas import tpu as pltpu
from jax.sharding import PartitionSpec as P

MESH = pl.DeviceIdType.MESH
NX, NY, NZ = 4, 8, 8
CAP = 14
SLOT = 16
NQ = 4
PER = 8
CHUNK = PER * CAP
ROWS = 224
DIM = 1024
SPAN = 1 << 17
CLASSES = NQ * PER
HELD = 3 * CHUNK


def eye(rows, lanes):
    return lax.broadcasted_iota(jnp.int32, (rows, lanes), 0) == lax.broadcasted_iota(
        jnp.int32, (rows, lanes), 1
    )


def column_of(row, rows):
    lanes = row.shape[1]
    zero = jnp.zeros((rows, lanes), row.dtype)
    spread = jnp.broadcast_to(row, (rows, lanes))
    return jnp.sum(jnp.where(eye(rows, lanes), spread, zero), axis=1, keepdims=True)


def contract_lanes(left, right):
    return lax.dot_general(
        left, right, (((1,), (1,)), ((), ())), preferred_element_type=jnp.float32
    )


def to_bf16(mask):
    return mask.astype(jnp.float32).astype(jnp.bfloat16)


def y_steps(n):
    return (n + 1) // 2 if n % 2 else (NY - n // 2) % NY


def z_steps(q):
    return (4 - q) % 4


FIRST = 48
FARTHEST = sorted(
    ((q, n) for q in range(NQ) for n in range(PER) if q or n),
    key=lambda slot: -(z_steps(slot[0]) + (slot[1] + 1) // 2),
)


def kernel(
    emb_hbm, cid_hbm, idx_hbm, out_ref,
    emb_ref, cid_ref, idx_ref, unit, send, recv, held, query, keys, key_cols, clu_cols, scores,
    best_k, best_q, part_out, part_in, final, back,
    in_sem, own_sem, a2a_send, a2a_recv, y_send, y_recv, k_send, k_recv, p_send, p_recv, b_send, b_recv,
):
    owner = lax.axis_index("owner")
    panel = lax.axis_index("panel")
    x, zh, core = owner // 8, (owner // 2) % 4, owner % 2
    zl, y = panel // 8, panel % 8
    z = zh * 2 + zl

    loads = [
        pltpu.make_async_copy(src, dst, in_sem.at[i])
        for i, (src, dst) in enumerate(
            ((cid_hbm, cid_ref), (idx_hbm, idx_ref), (emb_hbm, emb_ref))
        )
    ]
    for load in loads:
        load.start()

    def at(ax, ay, az, ac):
        return {"owner": (ax * 4 + az // 2) * 2 + ac, "panel": (az % 2) * 8 + ay}

    def along_x(step):
        return at((x + step + NX) % NX, y, z, core)

    def home(q, n):
        m = z_steps(q)
        up = jnp.where((z + m) % 2 == 0, m, NZ - m)
        return at(x, (y + y_steps(n)) % NY, (z + up) % NZ, core)

    def source(q, n):
        m = z_steps(q)
        up = jnp.where(z % 2 == 0, NZ - m, m)
        return at(x, (y - y_steps(n) + NY) % NY, (z + up) % NZ, core)

    pair_z = zh * 2 + 1 - zl
    pair, twin = at(x, y, pair_z, core), at(x, y, z, 1 - core)
    barrier = pltpu.get_barrier_semaphore()
    for q, n in FARTHEST:
        pl.semaphore_signal(barrier, inc=1, device_id=source(q, n), device_id_type=MESH)
    nearby = [along_x(-1), along_x(1), pair, twin]
    for peer in nearby:
        pl.semaphore_signal(barrier, inc=1, device_id=peer, device_id_type=MESH)

    for load in loads[:2]:
        load.wait()
    cid = cid_ref[...]
    residue = cid & (CLASSES - 1)
    dy = ((residue >> 2) - y) & (NY - 1)
    dz = (z - 2 * (residue & 3)) & (NZ - 1)
    member = jnp.where((dz == 0) | (dz > 4), (NZ - dz) & (NZ - 1), dz - 1)
    quarter = (4 - member) & 3
    place = jnp.where(dy <= 4, jnp.maximum(2 * dy - 1, 0), 2 * (NY - dy))
    offset = quarter * PER + place
    key = (cid >> 5) * SPAN + idx_ref[...] + 1
    offset_col = column_of(offset, ROWS)
    key_col = column_of(key, ROWS)
    first = lax.broadcasted_iota(jnp.int32, (ROWS, ROWS), 0)
    second = lax.broadcasted_iota(jnp.int32, (ROWS, ROWS), 1)
    equal = offset_col == offset
    rank = jnp.sum((equal & (first < second)).astype(jnp.int32), axis=0, keepdims=True)
    rank_col = jnp.sum((equal & (second < first)).astype(jnp.int32), axis=1, keepdims=True)
    lane = lax.broadcasted_iota(jnp.int32, (ROWS, 128), 1)
    digits = jnp.zeros((ROWS, 128), jnp.int32)
    for d, shift in enumerate((14, 7, 0)):
        digits = jnp.where(lane == SLOT * d + rank_col, (key_col >> shift) & 127, digits)
    digits = digits.astype(jnp.float32).astype(jnp.bfloat16)

    loads[2].wait()
    wide = emb_ref[...].astype(jnp.float32)
    inverse = lax.rsqrt(jnp.sum(wide * wide, axis=1, keepdims=True) + 1e-06)
    unit[...] = (wide * inverse).astype(jnp.bfloat16)
    def slotted(q):
        base = q * PER * SLOT
        slot = lax.broadcasted_iota(jnp.int32, (PER * SLOT, ROWS), 0) + base
        pick = to_bf16(slot == offset * SLOT + rank)
        pick_key = to_bf16(slot == offset * SLOT + CAP)
        rows = jnp.dot(pick, unit[...], preferred_element_type=jnp.float32)
        extra = jnp.dot(pick_key, digits, preferred_element_type=jnp.float32)
        send[base : base + PER * SLOT, 128:] = rows[:, 128:].astype(jnp.bfloat16)
        send[base : base + PER * SLOT, 0:128] = (rows[:, 0:128] + extra).astype(jnp.bfloat16)

    def give(q):
        for n in range(PER):
            if q or n:
                pltpu.make_async_remote_copy(
                    src_ref=send.at[pl.ds((q * PER + n) * SLOT, SLOT)],
                    dst_ref=recv.at[q, pl.ds(n * SLOT, SLOT)],
                    send_sem=a2a_send,
                    recv_sem=a2a_recv.at[q, n // 4],
                    device_id=home(q, n),
                    device_id_type=MESH,
                ).start()

    slotted(0)
    pl.semaphore_wait(barrier, CLASSES - 1 + len(nearby))
    for q in range(NQ):
        if q:
            slotted(q)
        give(q)
    recv[0, 0:SLOT, :] = send[0:SLOT, :]
    best_k[...] = jnp.full(best_k.shape, -1.0, jnp.float32)
    best_q[...] = jnp.full(best_q.shape, -1.0, jnp.float32)
    for q in range(NQ):
        for s in range(2):
            for base in (CHUNK, 128 + CHUNK):
                query[q, s, base : base + 128 - CHUNK, :] = jnp.zeros(
                    (128 - CHUNK, DIM), jnp.bfloat16
                )

    def part_of(q, j, h):
        start, size = (FIRST, CHUNK - FIRST) if h else (0, FIRST)
        if j < 2:
            return held.at[pl.ds(q * HELD + j * CHUNK + start, size)]
        return query.at[q, (j - 2) // 2, pl.ds((j - 2) % 2 * 128 + start, size)]

    copies = {}

    def pass_on(q, j, h, peer, to):
        copy = pltpu.make_async_remote_copy(
            src_ref=part_of(q, j, h), dst_ref=part_of(q, to, h),
            send_sem=y_send.at[q, to, h], recv_sem=y_recv.at[q, to, h],
            device_id=peer, device_id_type=MESH,
        )
        copy.start()
        copies[q, to, h] = copy
        if h:
            names = pltpu.make_async_remote_copy(
                src_ref=keys.at[q, j], dst_ref=keys.at[q, to],
                send_sem=k_send.at[q, to], recv_sem=k_recv.at[q, to],
                device_id=peer, device_id_type=MESH,
            )
            names.start()
            copies[q, to, 2] = names

    def arrived(q, j, h):
        copies[q, j, h].wait_recv()
        if h:
            copies[q, j, 2].wait_recv()

    def squeezer(start, size, below, width, nth=None):
        row = lax.broadcasted_iota(jnp.int32, (size, width), 0) + start
        col = lax.broadcasted_iota(jnp.int32, (size, width), 1) + below
        return to_bf16(col == row // CAP * SLOT + (row % CAP if nth is None else nth))

    squeeze = (
        squeezer(0, FIRST, 0, 4 * SLOT),
        squeezer(FIRST, CHUNK - FIRST, FIRST, PER * SLOT - FIRST),
    )
    key_rows = squeezer(0, CHUNK, 0, PER * SLOT, CAP)
    slot_col = lax.broadcasted_iota(jnp.int32, (CHUNK, PER * SLOT), 1)
    nth = lax.broadcasted_iota(jnp.int32, (CHUNK, PER * SLOT), 0) % CAP
    own_digit = (slot_col < 3 * SLOT) & (slot_col % SLOT == nth)
    digit_sum = to_bf16(
        lax.broadcasted_iota(jnp.int32, (8, 128), 1) // SLOT
        == lax.broadcasted_iota(jnp.int32, (8, 128), 0)
    )

    def own(q, h):
        skip = SLOT if q == 0 and h == 0 else 0
        landed = recv.at[q, pl.ds(h * 4 * SLOT + skip, 4 * SLOT - skip)]
        pltpu.make_async_copy(landed, landed, a2a_recv.at[q, h]).wait()
        base = q * HELD + CHUNK
        if h == 0:
            held[base : base + FIRST, :] = jnp.dot(
                squeeze[0], recv[q, 0 : 4 * SLOT, :], preferred_element_type=jnp.float32
            ).astype(jnp.bfloat16)
        else:
            held[base + FIRST : base + CHUNK, :] = jnp.dot(
                squeeze[1], recv[q, FIRST:, :], preferred_element_type=jnp.float32
            ).astype(jnp.bfloat16)
            spread = jnp.dot(key_rows, recv[q, :, 0:128], preferred_element_type=jnp.float32)
            spread = jnp.where(own_digit, spread, 0.0).astype(jnp.bfloat16)
            sums = contract_lanes(digit_sum, spread)
            value = sums[0:1] * 16384.0 + sums[1:2] * 128.0 + sums[2:3]
            keys[q, 1] = jnp.concatenate(
                [value, jnp.zeros((1, 128 - CHUNK), jnp.float32)], axis=1
            )
        pass_on(q, 1, h, along_x(-1), 2)
        pass_on(q, 1, h, along_x(1), 0)

    def own_copy(q, h):
        start, size = (FIRST, CHUNK - FIRST) if h else (0, FIRST)
        return pltpu.make_async_copy(
            part_of(q, 2, h),
            held.at[pl.ds(q * HELD + 2 * CHUNK + start, size)],
            own_sem.at[q, h],
        )

    def cross(q, h):
        arrived(q, 2, h)
        pass_on(q, 2, h, pair, 4)
        pass_on(q, 2, h, twin, 3)
        own_copy(q, h).start()

    def share(q, h):
        arrived(q, 4, h)
        pass_on(q, 4, h, twin, 5)

    def cluster_of(value):
        return jnp.floor((value - 1.0) * (1.0 / SPAN))

    def near(q):
        for h in range(2):
            arrived(q, 0, h)
            own_copy(q, h).wait()
        for j in range(3):
            column = jnp.broadcast_to(column_of(keys[q, j], CHUNK), (CHUNK, 128))
            base = q * HELD + j * CHUNK
            key_cols[base : base + CHUNK, :] = column
            clu_cols[base : base + CHUNK, :] = cluster_of(column)
        for h in range(2):
            arrived(q, 3, h)

    def far(q):
        for h in range(2):
            arrived(q, 5, h)

    def score(first, count, qq, s):
        rows = count * HELD
        scores[0:rows, :] = contract_lanes(
            held[first * HELD : first * HELD + rows, :], query[qq, s]
        )
        key_row = [keys[qq, 2 + 2 * s + i] for i in range(2)]
        clu_row = [cluster_of(row) for row in key_row]

        def one_chunk(k, tops):
            tops = list(tops)
            base = pl.multiple_of((first + k) * HELD, 8)
            for g in range(HELD // 8):
                at_rows = pl.ds(base + g * 8, 8)
                from_rows = pl.ds(pl.multiple_of(k * HELD, 8) + g * 8, 8)
                key_here = key_cols[at_rows, :]
                clu_here = clu_cols[at_rows, :]
                top = best_k[at_rows, :]
                for i in range(2):
                    value = scores[from_rows, i * 128 : (i + 1) * 128]
                    value = jnp.where(clu_here == clu_row[i], value, -1.0)
                    top = jnp.maximum(top, jnp.where(key_row[i] < key_here, value, -1.0))
                    if CHUNK <= g * 8 < 2 * CHUNK:
                        tops[i] = jnp.maximum(
                            tops[i], jnp.where(key_here < key_row[i], value, -1.0)
                        )
                best_k[at_rows, :] = top
            return tuple(tops)

        tops = tuple(best_q[qq, s, :, i * 128 : (i + 1) * 128] for i in range(2))
        tops = lax.fori_loop(0, count, one_chunk, tops)
        for i in range(2):
            best_q[qq, s, :, i * 128 : (i + 1) * 128] = tops[i]

    def score_one(k, qq, s):
        base = pl.multiple_of(k * HELD, 16)
        scores[0:HELD, :] = contract_lanes(held[pl.ds(base, HELD), :], query[qq, s])
        key_row = [keys[qq, 2 + 2 * s + i] for i in range(2)]
        clu_row = [cluster_of(row) for row in key_row]
        tops = [best_q[qq, s, :, i * 128 : (i + 1) * 128] for i in range(2)]
        for g in range(HELD // 8):
            at_rows = pl.ds(base + g * 8, 8)
            key_here = key_cols[at_rows, :]
            clu_here = clu_cols[at_rows, :]
            top = best_k[at_rows, :]
            for i in range(2):
                value = scores[g * 8 : g * 8 + 8, i * 128 : (i + 1) * 128]
                value = jnp.where(clu_here == clu_row[i], value, -1.0)
                top = jnp.maximum(top, jnp.where(key_row[i] < key_here, value, -1.0))
                if CHUNK <= g * 8 < 2 * CHUNK:
                    tops[i] = jnp.maximum(tops[i], jnp.where(key_here < key_row[i], value, -1.0))
            best_k[at_rows, :] = top
        for i in range(2):
            best_q[qq, s, :, i * 128 : (i + 1) * 128] = tops[i]

    def score_halves(first, count, start, stop):
        def step(t, carry):
            score(first, count, t // 2, t % 2)
            return carry

        lax.fori_loop(start, stop, step, 0)

    own(0, 0)
    own(0, 1)
    cross(0, 0)
    own(1, 0)
    cross(0, 1)
    own(1, 1)
    share(0, 0)
    own(2, 0)
    cross(1, 0)
    share(0, 1)
    cross(1, 1)
    own(2, 1)
    near(0)
    far(0)
    own(3, 0)
    cross(2, 0)
    share(1, 0)
    own(3, 1)
    cross(2, 1)
    share(1, 1)
    near(1)
    near(2)
    score_halves(0, 3, 0, 2)
    share(2, 0)
    cross(3, 0)
    far(1)
    share(2, 1)
    cross(3, 1)
    score_halves(0, 3, 2, 4)
    near(3)
    score_halves(3, 1, 0, 4)
    far(2)
    share(3, 0)
    score_halves(0, 4, 4, 6)
    score(0, 4, 3, 0)
    share(3, 1)
    far(3)
    def last(k, carry):
        score_one(k, 3, 1)
        return carry

    lax.fori_loop(0, NQ, last, 0)

    square = eye(CHUNK, 128)

    def over_query(q, j):
        base = q * HELD + j * CHUNK
        column = jnp.max(best_k[base : base + CHUNK, :], axis=1, keepdims=True)
        column = jnp.broadcast_to(column, (CHUNK, 128))
        return jnp.max(jnp.where(square, column, -1.0), axis=0, keepdims=True)

    for q in range(NQ):
        for u in range(4):
            lanes = slice(u % 2 * 128, u % 2 * 128 + 128)
            row = jnp.max(best_q[q, u // 2, :, lanes], axis=0, keepdims=True)
            if u == 0:
                row = jnp.maximum(row, over_query(q, 2))
            part_out[u, q : q + 1, :] = row
        part_out[4, q : q + 1, :] = over_query(q, 0)
    parts = []
    ahead = (x + 1) % NX
    for u, peer in enumerate((
        at(ahead, y, z, core), at(ahead, y, z, 1 - core),
        at(ahead, y, pair_z, core), at(ahead, y, pair_z, 1 - core), along_x(-1),
    )):
        part_out[u, NQ:8, :] = jnp.full((8 - NQ, 128), -1.0, jnp.float32)
        copy = pltpu.make_async_remote_copy(
            src_ref=part_out.at[u], dst_ref=part_in.at[u],
            send_sem=p_send.at[u], recv_sem=p_recv.at[u],
            device_id=peer, device_id_type=MESH,
        )
        copy.start()
        parts.append(copy)
    best = [over_query(q, 1) for q in range(NQ)]
    for u, copy in enumerate(parts):
        copy.wait_recv()
        best = [jnp.maximum(best[q], part_in[u, q : q + 1, :]) for q in range(NQ)]
    for q in range(NQ):
        final[q] = best[q]
    back[0] = best[0]

    for q, n in FARTHEST:
        pltpu.make_async_remote_copy(
            src_ref=final.at[q],
            dst_ref=back.at[q * PER + n],
            send_sem=b_send,
            recv_sem=b_recv,
            device_id=source(q, n),
            device_id_type=MESH,
        ).start()

    inbound = back.at[pl.ds(1, CLASSES - 1)]
    pltpu.make_async_copy(inbound, inbound, b_recv).wait()
    lane_row = lax.broadcasted_iota(jnp.int32, (1, 128), 1)
    hit = lax.broadcasted_iota(jnp.int32, (128, ROWS), 0) == place * CAP + rank
    result = jnp.zeros((1, ROWS), jnp.float32)
    for q in range(NQ):
        mine = jnp.zeros((1, 128), jnp.float32)
        for n in range(PER):
            mine = jnp.where(lane_row // CAP == n, back[q * PER + n], mine)
        column = jnp.broadcast_to(column_of(mine, 128), (128, ROWS))
        chosen = jnp.sum(jnp.where(hit, column, 0.0), axis=0, keepdims=True)
        result = jnp.where(quarter == q, chosen, result)
    out_ref[...] = result

    gone = send.at[pl.ds(SLOT, (CLASSES - 1) * SLOT)]
    pltpu.make_async_copy(gone, gone, a2a_send).wait()
    for copy in copies.values():
        copy.wait_send()
    for copy in parts:
        copy.wait_send()
    pltpu.make_async_copy(inbound, inbound, b_send).wait()


def per_device(embeddings, cluster_id, row_index):
    result = pl.pallas_call(
        kernel,
        out_shape=jax.ShapeDtypeStruct((1, ROWS), jnp.float32),
        in_specs=[pl.BlockSpec(memory_space=pl.ANY)] * 3,
        out_specs=pl.BlockSpec(memory_space=pltpu.VMEM),
        scratch_shapes=[
            pltpu.VMEM((ROWS, DIM), jnp.bfloat16),
            pltpu.VMEM((1, ROWS), jnp.int32),
            pltpu.VMEM((1, ROWS), jnp.int32),
            pltpu.VMEM((ROWS, DIM), jnp.bfloat16),
            pltpu.VMEM((CLASSES * SLOT, DIM), jnp.bfloat16),
            pltpu.VMEM((NQ, PER * SLOT, DIM), jnp.bfloat16),
            pltpu.VMEM((NQ * HELD, DIM), jnp.bfloat16),
            pltpu.VMEM((NQ, 2, 256, DIM), jnp.bfloat16),
            pltpu.VMEM((NQ, 6, 1, 128), jnp.float32),
            pltpu.VMEM((NQ * HELD, 128), jnp.float32),
            pltpu.VMEM((NQ * HELD, 128), jnp.float32),
            pltpu.VMEM((NQ * HELD, 256), jnp.float32),
            pltpu.VMEM((NQ * HELD, 128), jnp.float32),
            pltpu.VMEM((NQ, 2, 8, 256), jnp.float32),
            pltpu.VMEM((5, 8, 128), jnp.float32),
            pltpu.VMEM((5, 8, 128), jnp.float32),
            pltpu.VMEM((NQ, 1, 128), jnp.float32),
            pltpu.VMEM((CLASSES, 1, 128), jnp.float32),
            pltpu.SemaphoreType.DMA((3,)),
            pltpu.SemaphoreType.DMA((NQ, 2)),
            pltpu.SemaphoreType.DMA,
            pltpu.SemaphoreType.DMA((NQ, 2)),
            pltpu.SemaphoreType.DMA((NQ, 6, 2)),
            pltpu.SemaphoreType.DMA((NQ, 6, 2)),
            pltpu.SemaphoreType.DMA((NQ, 6)),
            pltpu.SemaphoreType.DMA((NQ, 6)),
            pltpu.SemaphoreType.DMA((5,)),
            pltpu.SemaphoreType.DMA((5,)),
            pltpu.SemaphoreType.DMA,
            pltpu.SemaphoreType.DMA,
        ],
        compiler_params=pltpu.CompilerParams(
            collective_id=0, has_side_effects=True, vmem_limit_bytes=62 * 1024 * 1024
        ),
    )(embeddings, cluster_id.reshape(1, ROWS), row_index.reshape(1, ROWS))
    return result.reshape(ROWS)


def solution(mesh):
    placed = (P(("owner", "panel"), None), P(("owner", "panel")), P(("owner", "panel")))
    return jax.shard_map(
        per_device, mesh=mesh, in_specs=placed, out_specs=P(("owner", "panel")), check_vma=False
    )
```

```python
import jax
import jax.numpy as jnp
from jax import lax
from jax.experimental import pallas as pl
from jax.experimental.pallas import tpu as pltpu
from jax.sharding import PartitionSpec as P

MESH = pl.DeviceIdType.MESH
NX, NY, NZ = 4, 8, 8
CAP = 14
SLOT = 16
NQ = 4
PER = 8
CHUNK = PER * CAP
ROWS = 224
DIM = 1024
SPAN = 1 << 17
CLASSES = NQ * PER
HELD = 3 * CHUNK


def eye(rows, lanes):
    return lax.broadcasted_iota(jnp.int32, (rows, lanes), 0) == lax.broadcasted_iota(
        jnp.int32, (rows, lanes), 1
    )


def column_of(row, rows):
    lanes = row.shape[1]
    zero = jnp.zeros((rows, lanes), row.dtype)
    spread = jnp.broadcast_to(row, (rows, lanes))
    return jnp.sum(jnp.where(eye(rows, lanes), spread, zero), axis=1, keepdims=True)


def contract_lanes(left, right):
    return lax.dot_general(
        left, right, (((1,), (1,)), ((), ())), preferred_element_type=jnp.float32
    )


def to_bf16(mask):
    return mask.astype(jnp.float32).astype(jnp.bfloat16)


def y_steps(n):
    return (n + 1) // 2 if n % 2 else (NY - n // 2) % NY


def z_steps(q):
    return (4 - q) % 4


FIRST = 48
TILES = 7
PACKED = TILES * 128
SPARE = PER * (SLOT - CAP)
FARTHEST = sorted(
    ((q, n) for q in range(NQ) for n in range(PER) if q or n),
    key=lambda slot: -(z_steps(slot[0]) + (slot[1] + 1) // 2),
)


def kernel(
    emb_hbm, cid_hbm, idx_hbm, out_ref,
    emb_ref, cid_ref, idx_ref, slots, unit, send, recv, key_out, key_in, held, query, keys, key_cols, clu_cols, scores,
    best_k, best_q, part_out, part_in, final, back,
    in_sem, own_sem, a2a_send, a2a_recv, n_send, n_recv, y_send, y_recv, k_send, k_recv, p_send, p_recv, b_send, b_recv,
):
    owner = lax.axis_index("owner")
    panel = lax.axis_index("panel")
    x, zh, core = owner // 8, (owner // 2) % 4, owner % 2
    zl, y = panel // 8, panel % 8
    z = zh * 2 + zl

    loads = [
        pltpu.make_async_copy(src, dst, in_sem.at[i])
        for i, (src, dst) in enumerate(
            ((cid_hbm, cid_ref), (idx_hbm, idx_ref), (emb_hbm, emb_ref))
        )
    ]
    for load in loads:
        load.start()

    def at(ax, ay, az, ac):
        return {"owner": (ax * 4 + az // 2) * 2 + ac, "panel": (az % 2) * 8 + ay}

    def along_x(step):
        return at((x + step + NX) % NX, y, z, core)

    def home(q, n):
        m = z_steps(q)
        up = jnp.where((z + m) % 2 == 0, m, NZ - m)
        return at(x, (y + y_steps(n)) % NY, (z + up) % NZ, core)

    def source(q, n):
        m = z_steps(q)
        up = jnp.where(z % 2 == 0, NZ - m, m)
        return at(x, (y - y_steps(n) + NY) % NY, (z + up) % NZ, core)

    pair_z = zh * 2 + 1 - zl
    pair, twin = at(x, y, pair_z, core), at(x, y, z, 1 - core)
    barrier = pltpu.get_barrier_semaphore()
    for q, n in FARTHEST:
        pl.semaphore_signal(barrier, inc=1, device_id=source(q, n), device_id_type=MESH)
    nearby = [along_x(-1), along_x(1), pair, twin]
    for peer in nearby:
        pl.semaphore_signal(barrier, inc=1, device_id=peer, device_id_type=MESH)

    for load in loads[:2]:
        load.wait()
    cid = cid_ref[...]
    residue = cid & (CLASSES - 1)
    dy = ((residue >> 2) - y) & (NY - 1)
    dz = (z - 2 * (residue & 3)) & (NZ - 1)
    member = jnp.where((dz == 0) | (dz > 4), (NZ - dz) & (NZ - 1), dz - 1)
    quarter = (4 - member) & 3
    place = jnp.where(dy <= 4, jnp.maximum(2 * dy - 1, 0), 2 * (NY - dy))
    offset = quarter * PER + place
    key = (cid >> 5) * SPAN + idx_ref[...] + 1
    offset_col = column_of(offset, ROWS)
    key_col = column_of(key, ROWS)
    first = lax.broadcasted_iota(jnp.int32, (ROWS, ROWS), 0)
    second = lax.broadcasted_iota(jnp.int32, (ROWS, ROWS), 1)
    equal = offset_col == offset
    rank = jnp.sum((equal & (first < second)).astype(jnp.int32), axis=0, keepdims=True)
    rank_col = jnp.sum((equal & (second < first)).astype(jnp.int32), axis=1, keepdims=True)
    slots[...] = jnp.zeros(slots.shape, jnp.int32)
    slots[:, 0:ROWS] = offset * SLOT + rank

    loads[2].wait()
    wide = emb_ref[...].astype(jnp.float32)
    inverse = lax.rsqrt(jnp.sum(wide * wide, axis=1, keepdims=True) + 1e-06)
    unit[0:ROWS, :] = (wide * inverse).astype(jnp.bfloat16)
    depth = ROWS + SPARE
    lane = lax.broadcasted_iota(jnp.int32, (1, depth), 1)
    extra = lane - ROWS
    extra = (extra >> 1) * SLOT + CAP + (extra & 1)
    row = lax.broadcasted_iota(jnp.int32, (TILES * SPARE, ROWS), 0)
    tail_slot = ((row & (SPARE - 1)) >> 1) * SLOT + (row >> 4) + (row & 1) * TILES
    plain = lax.broadcasted_iota(jnp.int32, (PER * SLOT, depth), 0)

    def slotted(q):
        base = q * PER * SLOT
        tails = jnp.dot(
            to_bf16(tail_slot == slots[:, 0:ROWS] - base),
            unit[0:ROWS, PACKED:], preferred_element_type=jnp.float32,
        ).astype(jnp.bfloat16)
        for t in range(TILES):
            unit[ROWS:depth, t * 128 : t * 128 + 128] = tails[t * SPARE : (t + 1) * SPARE]
        pick = plain == jnp.where(lane < ROWS, slots[:, 0:depth] - base, extra)
        send[base : base + PER * SLOT, :] = jnp.dot(
            to_bf16(pick), unit[:, 0:PACKED], preferred_element_type=jnp.float32
        ).astype(jnp.bfloat16)

    def give(q):
        for n in range(PER):
            if q or n:
                pltpu.make_async_remote_copy(
                    src_ref=send.at[pl.ds((q * PER + n) * SLOT, SLOT)],
                    dst_ref=recv.at[q, pl.ds(n * SLOT, SLOT)],
                    send_sem=a2a_send,
                    recv_sem=a2a_recv.at[q, n // 4],
                    device_id=home(q, n),
                    device_id_type=MESH,
                ).start()

    slotted(0)
    pl.semaphore_wait(barrier, CLASSES - 1 + len(nearby))
    def clear():
        best_k[...] = jnp.full(best_k.shape, -1.0, jnp.float32)
        best_q[...] = jnp.full(best_q.shape, -1.0, jnp.float32)
        for q in range(NQ):
            for s in range(2):
                for base in (CHUNK, 128 + CHUNK):
                    query[q, s, base : base + 128 - CHUNK, :] = jnp.zeros(
                        (128 - CHUNK, DIM), jnp.bfloat16
                    )

    def fill_keys():
        here = lax.broadcasted_iota(jnp.int32, (ROWS, 128), 1) == (
            (offset_col & (PER - 1)) * CAP + rank_col
        )
        ours = to_bf16(lax.broadcasted_iota(jnp.int32, (CLASSES, ROWS), 0) == offset)
        digits = [
            jnp.where(here, (key_col >> shift) & 127, 0).astype(jnp.float32).astype(jnp.bfloat16)
            for shift in (14, 7, 0)
        ]
        table = jnp.dot(
            ours, jnp.concatenate(digits, axis=1), preferred_element_type=jnp.float32
        )
        table = table[:, 0:128] * 16384.0 + table[:, 128:256] * 128.0 + table[:, 256:384]
        for k in range(CLASSES):
            key_out[k] = table[k : k + 1, :]
        key_in[0] = key_out[0]

    def give_keys(part):
        for q, n in FARTHEST[part * 8 : part * 8 + 8]:
            pltpu.make_async_remote_copy(
                src_ref=key_out.at[q * PER + n],
                dst_ref=key_in.at[q * PER + n],
                send_sem=n_send,
                recv_sem=n_recv,
                device_id=home(q, n),
                device_id_type=MESH,
            ).start()

    def part_of(q, j, h):
        start, size = (FIRST, CHUNK - FIRST) if h else (0, FIRST)
        if j < 2:
            return held.at[pl.ds(q * HELD + j * CHUNK + start, size)]
        return query.at[q, (j - 2) // 2, pl.ds((j - 2) % 2 * 128 + start, size)]

    copies = {}

    def pass_on(q, j, h, peer, to):
        copy = pltpu.make_async_remote_copy(
            src_ref=part_of(q, j, h), dst_ref=part_of(q, to, h),
            send_sem=y_send.at[q, to, h], recv_sem=y_recv.at[q, to, h],
            device_id=peer, device_id_type=MESH,
        )
        copy.start()
        copies[q, to, h] = copy

    def pass_keys(j, peer, to):
        copy = pltpu.make_async_remote_copy(
            src_ref=keys.at[j], dst_ref=keys.at[to],
            send_sem=k_send.at[to], recv_sem=k_recv.at[to],
            device_id=peer, device_id_type=MESH,
        )
        copy.start()
        copies["keys", to] = copy

    def arrived(q, j, h):
        copies[q, j, h].wait_recv()

    def squeezer(start, size, below, width, nth=None):
        row = lax.broadcasted_iota(jnp.int32, (size, width), 0) + start
        col = lax.broadcasted_iota(jnp.int32, (size, width), 1) + below
        return to_bf16(col == row // CAP * SLOT + (row % CAP if nth is None else nth))

    def unpacker(start, size, below, width):
        row = lax.broadcasted_iota(jnp.int32, (size + SPARE, width), 0)
        col = lax.broadcasted_iota(jnp.int32, (size + SPARE, width), 1) + below
        spare = row - size
        spare = (spare >> 1) * SLOT + CAP + (spare & 1)
        row = row + start
        main = col == jnp.where(row < start + size, row // CAP * SLOT + row % CAP, spare)
        row = lax.broadcasted_iota(jnp.int32, (size, TILES * SPARE), 0) + start
        col = lax.broadcasted_iota(jnp.int32, (size, TILES * SPARE), 1)
        tail = (row // CAP == (col & (SPARE - 1)) >> 1) & (
            row % CAP == (col >> 4) + (col & 1) * TILES
        )
        return below, width, to_bf16(main), to_bf16(tail)

    unpack = (
        unpacker(0, FIRST, 0, 4 * SLOT),
        unpacker(FIRST, CHUNK - FIRST, FIRST, PER * SLOT - FIRST),
    )

    def own(q, h):
        skip = SLOT if q == 0 and h == 0 else 0
        landed = recv.at[q, pl.ds(h * 4 * SLOT + skip, 4 * SLOT - skip)]
        pltpu.make_async_copy(landed, landed, a2a_recv.at[q, h]).wait()
        below, width, main, tail = unpack[h]
        size = tail.shape[0]
        base = q * HELD + CHUNK + h * FIRST
        rows = jnp.dot(
            main, recv[q, below : below + width, :], preferred_element_type=jnp.float32
        ).astype(jnp.bfloat16)
        held[base : base + size, 0:PACKED] = rows[0:size]
        last = jnp.concatenate(
            [rows[size:, t * 128 : t * 128 + 128] for t in range(TILES)], axis=0
        )
        held[base : base + size, PACKED:] = jnp.dot(
            tail, last, preferred_element_type=jnp.float32
        ).astype(jnp.bfloat16)
        pass_on(q, 1, h, along_x(-1), 2)
        pass_on(q, 1, h, along_x(1), 0)

    def own_keys():
        names = key_in.at[pl.ds(1, CLASSES - 1)]
        pltpu.make_async_copy(names, names, n_recv).wait()
        for q in range(NQ):
            total = key_in[q * PER]
            for n in range(1, PER):
                total = total + key_in[q * PER + n]
            keys[1, q] = total
        pass_keys(1, along_x(-1), 2)
        pass_keys(1, along_x(1), 0)

    def cross_keys():
        copies["keys", 2].wait_recv()
        pass_keys(2, pair, 4)
        pass_keys(2, twin, 3)

    def share_keys():
        copies["keys", 4].wait_recv()
        pass_keys(4, twin, 5)

    def own_copy(q, h):
        start, size = (FIRST, CHUNK - FIRST) if h else (0, FIRST)
        return pltpu.make_async_copy(
            part_of(q, 2, h),
            held.at[pl.ds(q * HELD + 2 * CHUNK + start, size)],
            own_sem.at[q, h],
        )

    def cross(q, h):
        arrived(q, 2, h)
        pass_on(q, 2, h, pair, 4)
        pass_on(q, 2, h, twin, 3)
        own_copy(q, h).start()

    def share(q, h):
        arrived(q, 4, h)
        pass_on(q, 4, h, twin, 5)

    def cluster_of(value):
        return jnp.floor((value - 1.0) * (1.0 / SPAN))

    def all_keys():
        for j in (0, 3, 5):
            copies["keys", j].wait_recv()
        for q in range(NQ):
            for j in range(3):
                column = jnp.broadcast_to(column_of(keys[j, q], CHUNK), (CHUNK, 128))
                base = q * HELD + j * CHUNK
                key_cols[base : base + CHUNK, :] = column
                clu_cols[base : base + CHUNK, :] = cluster_of(column)

    def near(q):
        for h in range(2):
            arrived(q, 0, h)
            own_copy(q, h).wait()
        for h in range(2):
            arrived(q, 3, h)

    def far(q):
        for h in range(2):
            arrived(q, 5, h)

    def score(first, count, qq, s):
        rows = count * HELD
        scores[0:rows, :] = contract_lanes(
            held[first * HELD : first * HELD + rows, :], query[qq, s]
        )
        key_row = [keys[2 + 2 * s + i, qq] for i in range(2)]
        clu_row = [cluster_of(row) for row in key_row]

        def one_chunk(k, tops):
            tops = list(tops)
            base = pl.multiple_of((first + k) * HELD, 8)
            for g in range(HELD // 8):
                at_rows = pl.ds(base + g * 8, 8)
                from_rows = pl.ds(pl.multiple_of(k * HELD, 8) + g * 8, 8)
                key_here = key_cols[at_rows, :]
                clu_here = clu_cols[at_rows, :]
                top = best_k[at_rows, :]
                for i in range(2):
                    value = scores[from_rows, i * 128 : (i + 1) * 128]
                    value = jnp.where(clu_here == clu_row[i], value, -1.0)
                    top = jnp.maximum(top, jnp.where(key_row[i] < key_here, value, -1.0))
                    if CHUNK <= g * 8 < 2 * CHUNK:
                        tops[i] = jnp.maximum(
                            tops[i], jnp.where(key_here < key_row[i], value, -1.0)
                        )
                best_k[at_rows, :] = top
            return tuple(tops)

        tops = tuple(best_q[qq, s, :, i * 128 : (i + 1) * 128] for i in range(2))
        tops = lax.fori_loop(0, count, one_chunk, tops)
        for i in range(2):
            best_q[qq, s, :, i * 128 : (i + 1) * 128] = tops[i]

    def score_rows(first, count, qq, s):
        rows = count * HELD
        base = pl.multiple_of(first * HELD, 16)
        scores[0:rows, :] = contract_lanes(held[pl.ds(base, rows), :], query[qq, s])
        key_row = [keys[2 + 2 * s + i, qq] for i in range(2)]
        clu_row = [cluster_of(row) for row in key_row]
        tops = [best_q[qq, s, :, i * 128 : (i + 1) * 128] for i in range(2)]
        for g in range(rows // 8):
            at_rows = pl.ds(base + g * 8, 8)
            key_here = key_cols[at_rows, :]
            clu_here = clu_cols[at_rows, :]
            top = best_k[at_rows, :]
            for i in range(2):
                value = scores[g * 8 : g * 8 + 8, i * 128 : (i + 1) * 128]
                value = jnp.where(clu_here == clu_row[i], value, -1.0)
                top = jnp.maximum(top, jnp.where(key_row[i] < key_here, value, -1.0))
                if CHUNK <= g * 8 % HELD < 2 * CHUNK:
                    tops[i] = jnp.maximum(tops[i], jnp.where(key_here < key_row[i], value, -1.0))
            best_k[at_rows, :] = top
        for i in range(2):
            best_q[qq, s, :, i * 128 : (i + 1) * 128] = tops[i]

    def score_halves(first, count, start, stop):
        def step(t, carry):
            score(first, count, t // 2, t % 2)
            return carry

        lax.fori_loop(start, stop, step, 0)

    def score_list(times, pick):
        def step(t, carry):
            score_rows(*pick(t))
            return carry

        lax.fori_loop(0, times, step, 0)

    give(0)
    recv[0, 0:SLOT, :] = send[0:SLOT, :]
    for q in range(1, NQ):
        slotted(q)
        give(q)
    own(0, 0)
    own(0, 1)
    fill_keys()
    give_keys(0)
    cross(0, 0)
    give_keys(1)
    own(1, 0)
    give_keys(2)
    cross(0, 1)
    give_keys(3)
    own(1, 1)
    clear()
    share(0, 0)
    own(2, 0)
    cross(1, 0)
    own_keys()
    share(0, 1)
    cross(1, 1)
    own(2, 1)
    cross_keys()
    near(0)
    far(0)
    own(3, 0)
    cross(2, 0)
    share_keys()
    share(1, 0)
    own(3, 1)
    cross(2, 1)
    all_keys()
    share(1, 1)
    near(1)
    near(2)
    score_halves(0, 3, 0, 2)
    share(2, 0)
    cross(3, 0)
    far(1)
    share(2, 1)
    cross(3, 1)
    score_halves(0, 3, 2, 4)
    near(3)
    score_halves(3, 1, 0, 4)
    far(2)
    share(3, 0)
    score_list(4, lambda t: (t % 2 * 2, 2, 2, t // 2))
    share(3, 1)
    score_list(2, lambda t: (t * 2, 2, 3, 0))
    far(3)
    def last(k, carry):
        score_rows(2 * k, 2, 3, 1)
        return carry

    lax.fori_loop(0, NQ // 2, last, 0)

    square = eye(CHUNK, 128)

    def over_query(q, j):
        base = q * HELD + j * CHUNK
        column = jnp.max(best_k[base : base + CHUNK, :], axis=1, keepdims=True)
        column = jnp.broadcast_to(column, (CHUNK, 128))
        return jnp.max(jnp.where(square, column, -1.0), axis=0, keepdims=True)

    for q in range(NQ):
        for u in range(4):
            lanes = slice(u % 2 * 128, u % 2 * 128 + 128)
            row = jnp.max(best_q[q, u // 2, :, lanes], axis=0, keepdims=True)
            if u == 0:
                row = jnp.maximum(row, over_query(q, 2))
            part_out[u, q : q + 1, :] = row
        part_out[4, q : q + 1, :] = over_query(q, 0)
    parts = []
    ahead = (x + 1) % NX
    for u, peer in enumerate((
        at(ahead, y, z, core), at(ahead, y, z, 1 - core),
        at(ahead, y, pair_z, core), at(ahead, y, pair_z, 1 - core), along_x(-1),
    )):
        part_out[u, NQ:8, :] = jnp.full((8 - NQ, 128), -1.0, jnp.float32)
        copy = pltpu.make_async_remote_copy(
            src_ref=part_out.at[u], dst_ref=part_in.at[u],
            send_sem=p_send.at[u], recv_sem=p_recv.at[u],
            device_id=peer, device_id_type=MESH,
        )
        copy.start()
        parts.append(copy)
    best = [over_query(q, 1) for q in range(NQ)]
    for u, copy in enumerate(parts):
        copy.wait_recv()
        best = [jnp.maximum(best[q], part_in[u, q : q + 1, :]) for q in range(NQ)]
    for q in range(NQ):
        final[q] = best[q]
    back[0] = best[0]

    for q, n in FARTHEST:
        pltpu.make_async_remote_copy(
            src_ref=final.at[q],
            dst_ref=back.at[q * PER + n],
            send_sem=b_send,
            recv_sem=b_recv,
            device_id=source(q, n),
            device_id_type=MESH,
        ).start()

    inbound = back.at[pl.ds(1, CLASSES - 1)]
    pltpu.make_async_copy(inbound, inbound, b_recv).wait()
    lane_row = lax.broadcasted_iota(jnp.int32, (1, 128), 1)
    hit = lax.broadcasted_iota(jnp.int32, (128, ROWS), 0) == place * CAP + rank
    result = jnp.zeros((1, ROWS), jnp.float32)
    for q in range(NQ):
        mine = jnp.zeros((1, 128), jnp.float32)
        for n in range(PER):
            mine = jnp.where(lane_row // CAP == n, back[q * PER + n], mine)
        column = jnp.broadcast_to(column_of(mine, 128), (128, ROWS))
        chosen = jnp.sum(jnp.where(hit, column, 0.0), axis=0, keepdims=True)
        result = jnp.where(quarter == q, chosen, result)
    out_ref[...] = result

    gone = send.at[pl.ds(SLOT, (CLASSES - 1) * SLOT)]
    pltpu.make_async_copy(gone, gone, a2a_send).wait()
    told = key_out.at[pl.ds(1, CLASSES - 1)]
    pltpu.make_async_copy(told, told, n_send).wait()
    for copy in copies.values():
        copy.wait_send()
    for copy in parts:
        copy.wait_send()
    pltpu.make_async_copy(inbound, inbound, b_send).wait()


def per_device(embeddings, cluster_id, row_index):
    result = pl.pallas_call(
        kernel,
        out_shape=jax.ShapeDtypeStruct((1, ROWS), jnp.float32),
        in_specs=[pl.BlockSpec(memory_space=pl.ANY)] * 3,
        out_specs=pl.BlockSpec(memory_space=pltpu.VMEM),
        scratch_shapes=[
            pltpu.VMEM((ROWS, DIM), jnp.bfloat16),
            pltpu.VMEM((1, ROWS), jnp.int32),
            pltpu.VMEM((1, ROWS), jnp.int32),
            pltpu.VMEM((1, 256), jnp.int32),
            pltpu.VMEM((ROWS + SPARE, DIM), jnp.bfloat16),
            pltpu.VMEM((CLASSES * SLOT, PACKED), jnp.bfloat16),
            pltpu.VMEM((NQ, PER * SLOT, PACKED), jnp.bfloat16),
            pltpu.VMEM((CLASSES, 1, 128), jnp.float32),
            pltpu.VMEM((CLASSES, 1, 128), jnp.float32),
            pltpu.VMEM((NQ * HELD, DIM), jnp.bfloat16),
            pltpu.VMEM((NQ, 2, 256, DIM), jnp.bfloat16),
            pltpu.VMEM((6, NQ, 1, 128), jnp.float32),
            pltpu.VMEM((NQ * HELD, 128), jnp.float32),
            pltpu.VMEM((NQ * HELD, 128), jnp.float32),
            pltpu.VMEM((NQ * HELD, 256), jnp.float32),
            pltpu.VMEM((NQ * HELD, 128), jnp.float32),
            pltpu.VMEM((NQ, 2, 8, 256), jnp.float32),
            pltpu.VMEM((5, 8, 128), jnp.float32),
            pltpu.VMEM((5, 8, 128), jnp.float32),
            pltpu.VMEM((NQ, 1, 128), jnp.float32),
            pltpu.VMEM((CLASSES, 1, 128), jnp.float32),
            pltpu.SemaphoreType.DMA((3,)),
            pltpu.SemaphoreType.DMA((NQ, 2)),
            pltpu.SemaphoreType.DMA,
            pltpu.SemaphoreType.DMA((NQ, 2)),
            pltpu.SemaphoreType.DMA,
            pltpu.SemaphoreType.DMA,
            pltpu.SemaphoreType.DMA((NQ, 6, 2)),
            pltpu.SemaphoreType.DMA((NQ, 6, 2)),
            pltpu.SemaphoreType.DMA((6,)),
            pltpu.SemaphoreType.DMA((6,)),
            pltpu.SemaphoreType.DMA((5,)),
            pltpu.SemaphoreType.DMA((5,)),
            pltpu.SemaphoreType.DMA,
            pltpu.SemaphoreType.DMA,
        ],
        compiler_params=pltpu.CompilerParams(
            collective_id=0, has_side_effects=True, vmem_limit_bytes=62 * 1024 * 1024
        ),
    )(embeddings, cluster_id.reshape(1, ROWS), row_index.reshape(1, ROWS))
    return result.reshape(ROWS)


def solution(mesh):
    placed = (P(("owner", "panel"), None), P(("owner", "panel")), P(("owner", "panel")))
    return jax.shard_map(
        per_device, mesh=mesh, in_specs=placed, out_specs=P(("owner", "panel")), check_vma=False
    )
```

```python
import jax
import jax.numpy as jnp
from jax import lax
from jax.experimental import pallas as pl
from jax.experimental.pallas import tpu as pltpu
from jax.sharding import PartitionSpec as P

MESH = pl.DeviceIdType.MESH
NX, NY, NZ = 4, 8, 8
CAP = 14
SLOT = 16
NQ = 4
PER = 8
CHUNK = PER * CAP
ROWS = 224
DIM = 1024
SPAN = 1 << 17
CLASSES = NQ * PER
HELD = 3 * CHUNK


def eye(rows, lanes):
    return lax.broadcasted_iota(jnp.int32, (rows, lanes), 0) == lax.broadcasted_iota(
        jnp.int32, (rows, lanes), 1
    )


def column_of(row, rows):
    lanes = row.shape[1]
    zero = jnp.zeros((rows, lanes), row.dtype)
    spread = jnp.broadcast_to(row, (rows, lanes))
    return jnp.sum(jnp.where(eye(rows, lanes), spread, zero), axis=1, keepdims=True)


def contract_lanes(left, right):
    return lax.dot_general(
        left, right, (((1,), (1,)), ((), ())), preferred_element_type=jnp.float32
    )


def to_bf16(mask):
    return mask.astype(jnp.float32).astype(jnp.bfloat16)


def y_steps(n):
    return (n + 1) // 2 if n % 2 else (NY - n // 2) % NY


def z_steps(q):
    return (4 - q) % 4


FIRST = 48
TILES = 7
PACKED = TILES * 128
SPARE = PER * (SLOT - CAP)
FARTHEST = sorted(
    ((q, n) for q in range(NQ) for n in range(PER) if q or n),
    key=lambda slot: -(z_steps(slot[0]) + (slot[1] + 1) // 2),
)


def held_row(q, j):
    if j == 1:
        return q * CHUNK
    return NQ * CHUNK + (NQ - 1 - q) * 2 * CHUNK + j // 2 * CHUNK


def kernel(
    emb_hbm, cid_hbm, idx_hbm, out_ref,
    emb_ref, cid_ref, idx_ref, slots, unit, send, recv, key_out, key_in, held, query, keys, key_cols, clu_cols, scores,
    best_k, best_q, part_out, part_in, final, back,
    in_sem, own_sem, a2a_send, a2a_recv, n_send, n_recv, y_send, y_recv, k_send, k_recv, p_send, p_recv, b_send, b_recv,
):
    owner = lax.axis_index("owner")
    panel = lax.axis_index("panel")
    x, zh, core = owner // 8, (owner // 2) % 4, owner % 2
    zl, y = panel // 8, panel % 8
    z = zh * 2 + zl

    loads = [
        pltpu.make_async_copy(src, dst, in_sem.at[i])
        for i, (src, dst) in enumerate(
            ((cid_hbm, cid_ref), (idx_hbm, idx_ref), (emb_hbm, emb_ref))
        )
    ]
    for load in loads:
        load.start()

    def at(ax, ay, az, ac):
        return {"owner": (ax * 4 + az // 2) * 2 + ac, "panel": (az % 2) * 8 + ay}

    def along_x(step):
        return at((x + step + NX) % NX, y, z, core)

    def home(q, n):
        m = z_steps(q)
        up = jnp.where((z + m) % 2 == 0, m, NZ - m)
        return at(x, (y + y_steps(n)) % NY, (z + up) % NZ, core)

    def source(q, n):
        m = z_steps(q)
        up = jnp.where(z % 2 == 0, NZ - m, m)
        return at(x, (y - y_steps(n) + NY) % NY, (z + up) % NZ, core)

    pair_z = zh * 2 + 1 - zl
    pair, twin = at(x, y, pair_z, core), at(x, y, z, 1 - core)
    barrier = pltpu.get_barrier_semaphore()
    for q, n in FARTHEST:
        pl.semaphore_signal(barrier, inc=1, device_id=source(q, n), device_id_type=MESH)
    nearby = [along_x(-1), along_x(1), pair, twin]
    for peer in nearby:
        pl.semaphore_signal(barrier, inc=1, device_id=peer, device_id_type=MESH)

    for load in loads[:2]:
        load.wait()
    cid = cid_ref[...]
    residue = cid & (CLASSES - 1)
    dy = ((residue >> 2) - y) & (NY - 1)
    dz = (z - 2 * (residue & 3)) & (NZ - 1)
    member = jnp.where((dz == 0) | (dz > 4), (NZ - dz) & (NZ - 1), dz - 1)
    quarter = (4 - member) & 3
    place = jnp.where(dy <= 4, jnp.maximum(2 * dy - 1, 0), 2 * (NY - dy))
    offset = quarter * PER + place
    key = (cid >> 5) * SPAN + idx_ref[...] + 1
    offset_col = column_of(offset, ROWS)
    key_col = column_of(key, ROWS)
    first = lax.broadcasted_iota(jnp.int32, (ROWS, ROWS), 0)
    second = lax.broadcasted_iota(jnp.int32, (ROWS, ROWS), 1)
    equal = offset_col == offset
    rank = jnp.sum((equal & (first < second)).astype(jnp.int32), axis=0, keepdims=True)
    rank_col = jnp.sum((equal & (second < first)).astype(jnp.int32), axis=1, keepdims=True)
    slots[...] = jnp.zeros(slots.shape, jnp.int32)
    slots[:, 0:ROWS] = offset * SLOT + rank

    loads[2].wait()
    wide = emb_ref[...].astype(jnp.float32)
    inverse = lax.rsqrt(jnp.sum(wide * wide, axis=1, keepdims=True) + 1e-06)
    unit[0:ROWS, :] = (wide * inverse).astype(jnp.bfloat16)
    depth = ROWS + SPARE
    lane = lax.broadcasted_iota(jnp.int32, (1, depth), 1)
    extra = lane - ROWS
    extra = (extra >> 1) * SLOT + CAP + (extra & 1)
    row = lax.broadcasted_iota(jnp.int32, (TILES * SPARE, ROWS), 0)
    tail_slot = ((row & (SPARE - 1)) >> 1) * SLOT + (row >> 4) + (row & 1) * TILES
    plain = lax.broadcasted_iota(jnp.int32, (PER * SLOT, depth), 0)

    def slotted(q):
        base = q * PER * SLOT
        tails = jnp.dot(
            to_bf16(tail_slot == slots[:, 0:ROWS] - base),
            unit[0:ROWS, PACKED:], preferred_element_type=jnp.float32,
        ).astype(jnp.bfloat16)
        for t in range(TILES):
            unit[ROWS:depth, t * 128 : t * 128 + 128] = tails[t * SPARE : (t + 1) * SPARE]
        pick = plain == jnp.where(lane < ROWS, slots[:, 0:depth] - base, extra)
        send[base : base + PER * SLOT, :] = jnp.dot(
            to_bf16(pick), unit[:, 0:PACKED], preferred_element_type=jnp.float32
        ).astype(jnp.bfloat16)

    def give(q):
        for n in range(PER):
            if q or n:
                pltpu.make_async_remote_copy(
                    src_ref=send.at[pl.ds((q * PER + n) * SLOT, SLOT)],
                    dst_ref=recv.at[q, pl.ds(n * SLOT, SLOT)],
                    send_sem=a2a_send,
                    recv_sem=a2a_recv.at[q, n // 4],
                    device_id=home(q, n),
                    device_id_type=MESH,
                ).start()

    slotted(0)
    pl.semaphore_wait(barrier, CLASSES - 1 + len(nearby))
    def clear():
        best_k[...] = jnp.full(best_k.shape, -1.0, jnp.float32)
        best_q[...] = jnp.full(best_q.shape, -1.0, jnp.float32)
        for q in range(NQ):
            for s in range(2):
                for base in (CHUNK, 128 + CHUNK):
                    query[q, s, base : base + 128 - CHUNK, :] = jnp.zeros(
                        (128 - CHUNK, DIM), jnp.bfloat16
                    )

    def fill_keys():
        here = lax.broadcasted_iota(jnp.int32, (ROWS, 128), 1) == (
            (offset_col & (PER - 1)) * CAP + rank_col
        )
        ours = to_bf16(lax.broadcasted_iota(jnp.int32, (CLASSES, ROWS), 0) == offset)
        digits = [
            jnp.where(here, (key_col >> shift) & 127, 0).astype(jnp.float32).astype(jnp.bfloat16)
            for shift in (14, 7, 0)
        ]
        table = jnp.dot(
            ours, jnp.concatenate(digits, axis=1), preferred_element_type=jnp.float32
        )
        table = table[:, 0:128] * 16384.0 + table[:, 128:256] * 128.0 + table[:, 256:384]
        for k in range(CLASSES):
            key_out[k] = table[k : k + 1, :]
        key_in[0] = key_out[0]

    def give_keys(part):
        for q, n in FARTHEST[part * 8 : part * 8 + 8]:
            pltpu.make_async_remote_copy(
                src_ref=key_out.at[q * PER + n],
                dst_ref=key_in.at[q * PER + n],
                send_sem=n_send,
                recv_sem=n_recv,
                device_id=home(q, n),
                device_id_type=MESH,
            ).start()

    def part_of(q, j, h):
        start, size = (FIRST, CHUNK - FIRST) if h else (0, FIRST)
        if j < 2:
            return held.at[pl.ds(held_row(q, j) + start, size)]
        return query.at[q, (j - 2) // 2, pl.ds((j - 2) % 2 * 128 + start, size)]

    copies = {}

    def pass_on(q, j, h, peer, to):
        copy = pltpu.make_async_remote_copy(
            src_ref=part_of(q, j, h), dst_ref=part_of(q, to, h),
            send_sem=y_send.at[q, to, h], recv_sem=y_recv.at[q, to, h],
            device_id=peer, device_id_type=MESH,
        )
        copy.start()
        copies[q, to, h] = copy

    def pass_keys(j, peer, to):
        copy = pltpu.make_async_remote_copy(
            src_ref=keys.at[j], dst_ref=keys.at[to],
            send_sem=k_send.at[to], recv_sem=k_recv.at[to],
            device_id=peer, device_id_type=MESH,
        )
        copy.start()
        copies["keys", to] = copy

    def arrived(q, j, h):
        copies[q, j, h].wait_recv()

    def squeezer(start, size, below, width, nth=None):
        row = lax.broadcasted_iota(jnp.int32, (size, width), 0) + start
        col = lax.broadcasted_iota(jnp.int32, (size, width), 1) + below
        return to_bf16(col == row // CAP * SLOT + (row % CAP if nth is None else nth))

    def unpacker(start, size, below, width):
        row = lax.broadcasted_iota(jnp.int32, (size + SPARE, width), 0)
        col = lax.broadcasted_iota(jnp.int32, (size + SPARE, width), 1) + below
        spare = row - size
        spare = (spare >> 1) * SLOT + CAP + (spare & 1)
        row = row + start
        main = col == jnp.where(row < start + size, row // CAP * SLOT + row % CAP, spare)
        row = lax.broadcasted_iota(jnp.int32, (size, TILES * SPARE), 0) + start
        col = lax.broadcasted_iota(jnp.int32, (size, TILES * SPARE), 1)
        tail = (row // CAP == (col & (SPARE - 1)) >> 1) & (
            row % CAP == (col >> 4) + (col & 1) * TILES
        )
        return below, width, to_bf16(main), to_bf16(tail)

    unpack = (
        unpacker(0, FIRST, 0, 4 * SLOT),
        unpacker(FIRST, CHUNK - FIRST, FIRST, PER * SLOT - FIRST),
    )

    def own(q, h):
        skip = SLOT if q == 0 and h == 0 else 0
        landed = recv.at[q, pl.ds(h * 4 * SLOT + skip, 4 * SLOT - skip)]
        pltpu.make_async_copy(landed, landed, a2a_recv.at[q, h]).wait()
        below, width, main, tail = unpack[h]
        size = tail.shape[0]
        base = held_row(q, 1) + h * FIRST
        rows = jnp.dot(
            main, recv[q, below : below + width, :], preferred_element_type=jnp.float32
        ).astype(jnp.bfloat16)
        held[base : base + size, 0:PACKED] = rows[0:size]
        last = jnp.concatenate(
            [rows[size:, t * 128 : t * 128 + 128] for t in range(TILES)], axis=0
        )
        held[base : base + size, PACKED:] = jnp.dot(
            tail, last, preferred_element_type=jnp.float32
        ).astype(jnp.bfloat16)
        pass_on(q, 1, h, along_x(-1), 2)
        pass_on(q, 1, h, along_x(1), 0)

    def own_keys():
        names = key_in.at[pl.ds(1, CLASSES - 1)]
        pltpu.make_async_copy(names, names, n_recv).wait()
        for q in range(NQ):
            total = key_in[q * PER]
            for n in range(1, PER):
                total = total + key_in[q * PER + n]
            keys[1, q] = total
        pass_keys(1, along_x(-1), 2)
        pass_keys(1, along_x(1), 0)

    def cross_keys():
        copies["keys", 2].wait_recv()
        pass_keys(2, pair, 4)
        pass_keys(2, twin, 3)

    def share_keys():
        copies["keys", 4].wait_recv()
        pass_keys(4, twin, 5)

    def own_copy(q, h):
        start, size = (FIRST, CHUNK - FIRST) if h else (0, FIRST)
        return pltpu.make_async_copy(
            part_of(q, 2, h),
            held.at[pl.ds(held_row(q, 2) + start, size)],
            own_sem.at[q, h],
        )

    def cross(q, h):
        arrived(q, 2, h)
        pass_on(q, 2, h, pair, 4)
        pass_on(q, 2, h, twin, 3)
        own_copy(q, h).start()

    def share(q, h):
        arrived(q, 4, h)
        pass_on(q, 4, h, twin, 5)

    def cluster_of(value):
        return jnp.floor((value - 1.0) * (1.0 / SPAN))

    def all_keys():
        for j in (0, 3, 5):
            copies["keys", j].wait_recv()
        for q in range(NQ):
            for j in range(3):
                column = jnp.broadcast_to(column_of(keys[j, q], CHUNK), (CHUNK, 128))
                base = held_row(q, j)
                key_cols[base : base + CHUNK, :] = column
                clu_cols[base : base + CHUNK, :] = cluster_of(column)

    def near(q):
        for h in range(2):
            arrived(q, 0, h)
            own_copy(q, h).wait()
        for h in range(2):
            arrived(q, 3, h)

    def far(q):
        for h in range(2):
            arrived(q, 5, h)

    def score(first, rows, qq, s):
        scores[0:rows, :] = contract_lanes(held[first : first + rows, :], query[qq, s])
        key_row = [keys[2 + 2 * s + i, qq] for i in range(2)]
        clu_row = [cluster_of(row) for row in key_row]
        tops = [best_q[qq, s, :, i * 128 : (i + 1) * 128] for i in range(2)]
        for g in range(rows // 8):
            at_rows = slice(first + g * 8, first + g * 8 + 8)
            key_here = key_cols[at_rows, :]
            clu_here = clu_cols[at_rows, :]
            top = best_k[at_rows, :]
            for i in range(2):
                value = scores[g * 8 : g * 8 + 8, i * 128 : (i + 1) * 128]
                value = jnp.where(clu_here == clu_row[i], value, -1.0)
                top = jnp.maximum(top, jnp.where(key_row[i] < key_here, value, -1.0))
                tops[i] = jnp.maximum(tops[i], jnp.where(key_here < key_row[i], value, -1.0))
            best_k[at_rows, :] = top
        for i in range(2):
            best_q[qq, s, :, i * 128 : (i + 1) * 128] = tops[i]

    def score_all(times, pick, *spans):
        def step(t, carry):
            for first, rows in spans:
                score(first, rows, *pick(t))
            return carry

        lax.fori_loop(0, times, step, 0)

    give(0)
    recv[0, 0:SLOT, :] = send[0:SLOT, :]
    for q in range(1, NQ):
        slotted(q)
        give(q)
    own(0, 0)
    own(0, 1)
    fill_keys()
    give_keys(0)
    cross(0, 0)
    give_keys(1)
    own(1, 0)
    give_keys(2)
    cross(0, 1)
    give_keys(3)
    own(1, 1)
    clear()
    share(0, 0)
    own(2, 0)
    cross(1, 0)
    own_keys()
    share(0, 1)
    cross(1, 1)
    own(2, 1)
    cross_keys()
    near(0)
    far(0)
    own(3, 0)
    cross(2, 0)
    share_keys()
    share(1, 0)
    own(3, 1)
    cross(2, 1)
    all_keys()
    share(1, 1)
    near(1)
    near(2)
    score_all(2, lambda t: (0, t), (0, HELD), (2 * HELD, 2 * HELD))
    share(2, 0)
    cross(3, 0)
    far(1)
    share(2, 1)
    cross(3, 1)
    score_all(2, lambda t: (1, t), (0, HELD), (2 * HELD, 4 * CHUNK))
    near(3)
    score_all(4, lambda t: (t // 2, t % 2), (HELD, HELD))
    far(2)
    share(3, 0)
    score_all(2, lambda t: (2, t), (0, 4 * CHUNK), (4 * CHUNK, 4 * CHUNK))
    share(3, 1)
    score(0, 2 * HELD, 3, 0)
    far(3)
    score(0, 2 * HELD, 3, 1)

    square = eye(CHUNK, 128)

    def over_query(q, j):
        base = held_row(q, j)
        column = jnp.max(best_k[base : base + CHUNK, :], axis=1, keepdims=True)
        column = jnp.broadcast_to(column, (CHUNK, 128))
        return jnp.max(jnp.where(square, column, -1.0), axis=0, keepdims=True)

    for q in range(NQ):
        for u in range(4):
            lanes = slice(u % 2 * 128, u % 2 * 128 + 128)
            row = jnp.max(best_q[q, u // 2, :, lanes], axis=0, keepdims=True)
            if u == 0:
                row = jnp.maximum(row, over_query(q, 2))
            part_out[u, q : q + 1, :] = row
        part_out[4, q : q + 1, :] = over_query(q, 0)
    parts = []
    ahead = (x + 1) % NX
    for u, peer in enumerate((
        at(ahead, y, z, core), at(ahead, y, z, 1 - core),
        at(ahead, y, pair_z, core), at(ahead, y, pair_z, 1 - core), along_x(-1),
    )):
        part_out[u, NQ:8, :] = jnp.full((8 - NQ, 128), -1.0, jnp.float32)
        copy = pltpu.make_async_remote_copy(
            src_ref=part_out.at[u], dst_ref=part_in.at[u],
            send_sem=p_send.at[u], recv_sem=p_recv.at[u],
            device_id=peer, device_id_type=MESH,
        )
        copy.start()
        parts.append(copy)
    best = [over_query(q, 1) for q in range(NQ)]
    for u, copy in enumerate(parts):
        copy.wait_recv()
        best = [jnp.maximum(best[q], part_in[u, q : q + 1, :]) for q in range(NQ)]
    for q in range(NQ):
        final[q] = best[q]
    back[0] = best[0]

    for q, n in FARTHEST:
        pltpu.make_async_remote_copy(
            src_ref=final.at[q],
            dst_ref=back.at[q * PER + n],
            send_sem=b_send,
            recv_sem=b_recv,
            device_id=source(q, n),
            device_id_type=MESH,
        ).start()

    inbound = back.at[pl.ds(1, CLASSES - 1)]
    pltpu.make_async_copy(inbound, inbound, b_recv).wait()
    lane_row = lax.broadcasted_iota(jnp.int32, (1, 128), 1)
    hit = lax.broadcasted_iota(jnp.int32, (128, ROWS), 0) == place * CAP + rank
    result = jnp.zeros((1, ROWS), jnp.float32)
    for q in range(NQ):
        mine = jnp.zeros((1, 128), jnp.float32)
        for n in range(PER):
            mine = jnp.where(lane_row // CAP == n, back[q * PER + n], mine)
        column = jnp.broadcast_to(column_of(mine, 128), (128, ROWS))
        chosen = jnp.sum(jnp.where(hit, column, 0.0), axis=0, keepdims=True)
        result = jnp.where(quarter == q, chosen, result)
    out_ref[...] = result

    gone = send.at[pl.ds(SLOT, (CLASSES - 1) * SLOT)]
    pltpu.make_async_copy(gone, gone, a2a_send).wait()
    told = key_out.at[pl.ds(1, CLASSES - 1)]
    pltpu.make_async_copy(told, told, n_send).wait()
    for copy in copies.values():
        copy.wait_send()
    for copy in parts:
        copy.wait_send()
    pltpu.make_async_copy(inbound, inbound, b_send).wait()


def per_device(embeddings, cluster_id, row_index):
    result = pl.pallas_call(
        kernel,
        out_shape=jax.ShapeDtypeStruct((1, ROWS), jnp.float32),
        in_specs=[pl.BlockSpec(memory_space=pl.ANY)] * 3,
        out_specs=pl.BlockSpec(memory_space=pltpu.VMEM),
        scratch_shapes=[
            pltpu.VMEM((ROWS, DIM), jnp.bfloat16),
            pltpu.VMEM((1, ROWS), jnp.int32),
            pltpu.VMEM((1, ROWS), jnp.int32),
            pltpu.VMEM((1, 256), jnp.int32),
            pltpu.VMEM((ROWS + SPARE, DIM), jnp.bfloat16),
            pltpu.VMEM((CLASSES * SLOT, PACKED), jnp.bfloat16),
            pltpu.VMEM((NQ, PER * SLOT, PACKED), jnp.bfloat16),
            pltpu.VMEM((CLASSES, 1, 128), jnp.float32),
            pltpu.VMEM((CLASSES, 1, 128), jnp.float32),
            pltpu.VMEM((NQ * HELD, DIM), jnp.bfloat16),
            pltpu.VMEM((NQ, 2, 256, DIM), jnp.bfloat16),
            pltpu.VMEM((6, NQ, 1, 128), jnp.float32),
            pltpu.VMEM((NQ * HELD, 128), jnp.float32),
            pltpu.VMEM((NQ * HELD, 128), jnp.float32),
            pltpu.VMEM((2 * HELD, 256), jnp.float32),
            pltpu.VMEM((NQ * HELD, 128), jnp.float32),
            pltpu.VMEM((NQ, 2, 8, 256), jnp.float32),
            pltpu.VMEM((5, 8, 128), jnp.float32),
            pltpu.VMEM((5, 8, 128), jnp.float32),
            pltpu.VMEM((NQ, 1, 128), jnp.float32),
            pltpu.VMEM((CLASSES, 1, 128), jnp.float32),
            pltpu.SemaphoreType.DMA((3,)),
            pltpu.SemaphoreType.DMA((NQ, 2)),
            pltpu.SemaphoreType.DMA,
            pltpu.SemaphoreType.DMA((NQ, 2)),
            pltpu.SemaphoreType.DMA,
            pltpu.SemaphoreType.DMA,
            pltpu.SemaphoreType.DMA((NQ, 6, 2)),
            pltpu.SemaphoreType.DMA((NQ, 6, 2)),
            pltpu.SemaphoreType.DMA((6,)),
            pltpu.SemaphoreType.DMA((6,)),
            pltpu.SemaphoreType.DMA((5,)),
            pltpu.SemaphoreType.DMA((5,)),
            pltpu.SemaphoreType.DMA,
            pltpu.SemaphoreType.DMA,
        ],
        compiler_params=pltpu.CompilerParams(
            collective_id=0, has_side_effects=True, vmem_limit_bytes=62 * 1024 * 1024
        ),
    )(embeddings, cluster_id.reshape(1, ROWS), row_index.reshape(1, ROWS))
    return result.reshape(ROWS)


def solution(mesh):
    placed = (P(("owner", "panel"), None), P(("owner", "panel")), P(("owner", "panel")))
    return jax.shard_map(
        per_device, mesh=mesh, in_specs=placed, out_specs=P(("owner", "panel")), check_vma=False
    )
```
